256 devices in a mesh: seq: 8 (over x, core), tensor: 8 (over z), dp: 4 (over y).
Axes of the slice: x: 4, y: 4, z: 8, core: 2. Of those that a mesh axis runs over, the one named last changes fastest.
Arguments:
- span_act: bfloat16 [8192, 8192], P(('seq', 'dp'), 'tensor'), may hold values from -6 to 6
- q_weight: bfloat16 [8192, 4096], P(('seq', 'dp'), 'tensor'), may hold values from -0.0625 to 0.0625
- out_grad: bfloat16 [8192, 4096], P(('seq', 'dp'), 'tensor'), may hold values from -6 to 6
- neighbour_kv: bfloat16 [256, 2, 256, 4096], P(('seq', 'dp'), None, None, 'tensor'), may hold values from -210 to 210
- neighbour_ids: int32 [256, 256], P(('seq', 'dp')), may hold values from 0 to 255999, as said below
- owner: int32 [128], replicated, may hold values from 0 to 7, as said below
Outputs:
- act_grad: bfloat16 [8192, 8192], P(('seq', 'dp'), 'tensor')
- weight_grad: float32 [8192, 4096], P(('seq', 'dp'), 'tensor')
- kv_grad: bfloat16 [256, 2, 256, 4096], P(('seq', 'dp'), None, None, 'tensor')
The draws below stay inside these ranges and needn't reach their ends.
Inputs may be any that keep to these rules, and one draw needn't show every extreme that they name: owner[c] is the owner's index along seq within span c's own dp group. Of the 4 spans of one home block at most 1 name the same owner, and in each dp group some owner is named by 1 spans of every home block. `neighbour_ids`: each of the 2 neighbours of a slot takes 128 consecutive positions; its ids are positive on a leading run of 32 to 128 positions and 0 (padding) after it. Slots that no span names are never read.
All inputs are finite; a program needn't handle non-finite values.
Results may differ from the reference program's by a relative error of at most 0.022.
The reference program's roundings to bfloat16 on the way count: a program that leaves them out, or rounds other values in their place, can miss the bound.
Values may be sent and summed in bfloat16 or wider, within the bound.
A program may use at most 128 MiB of HBM per device.

```python
import jax
import jax.numpy as jnp
from jax import lax

D = 8192
HD = 128
SPAN = 64
NEIGH = 2
NLEN = 128
VOCAB = 256000
CH_DEV = 4
PAIR = 1
CAP = 8
KEYS = 256
HW = 4096
TOK_DEV = 256
TOKENS = 8192
SPANS = 128
SLOTS = 256
N_SEQ = 8
N_TENSOR = 8
N_DP = 4


def draw_neighbour_kv(key, part):
    key = jax.random.fold_in(key, 33)
    shape = (SLOTS, 2, KEYS, HW)
    base = jax.random.normal(jax.random.fold_in(key, 1), shape, jnp.float32)
    return base.astype(jnp.bfloat16)


def draw_neighbour_ids(key, part):
    key = jax.random.fold_in(key, 22)
    lengths = jax.random.randint(jax.random.fold_in(key, 1), (SLOTS, NEIGH), NLEN // 4, NLEN + 1)
    lengths = lengths.at[0, NEIGH - 1].set(NLEN // 4)
    position = jnp.arange(NLEN)
    alive = position[None, None, :] < lengths[:, :, None]
    tokens = jax.random.randint(jax.random.fold_in(key, 2), (SLOTS, NEIGH, NLEN), 1, VOCAB)
    tokens = jnp.where(alive, tokens, 0).reshape(SLOTS, KEYS)
    tokens = tokens.at[0, 0].set(VOCAB - 1)
    return tokens.astype(jnp.int32)


def draw_owner(key, part):
    key = jax.random.fold_in(key, 11)
    blocks = N_SEQ * N_DP
    hottest = jax.random.randint(jax.random.fold_in(key, 1), (N_DP,), 0, N_SEQ)

    def one_block(block):
        sub = jax.random.fold_in(key, block + 100)
        chosen = hottest[block % N_DP]
        others = (chosen + 1 + jnp.arange((N_SEQ - 1) * PAIR) // PAIR) % N_SEQ
        others = jax.random.permutation(jax.random.fold_in(sub, 1), others)
        picks = jnp.concatenate([jnp.full((PAIR,), chosen), others[:CH_DEV - PAIR]])
        order = jax.random.permutation(jax.random.fold_in(sub, 2), CH_DEV)
        return picks[order]
    return jax.vmap(one_block)(jnp.arange(blocks)).reshape(-1).astype(jnp.int32)


def raised(result, key, source, target, shards_of, factor):
    owner, partner = [(jnp.arange(result.shape[axis_at]) // (result.shape[axis_at] // shards_of)).reshape([-1 if axis == axis_at else 1 for axis in range(result.ndim)]) for axis_at in (source, target)]
    chosen = jax.random.permutation(key, shards_of)[partner]
    strong = (owner == chosen) | (owner == (partner + shards_of // 2) % shards_of)
    return jnp.where(strong, factor * result, result)


def block_scale(rng, shape, shards, smallest, top_value):
    factor_of, own = 1.0, jax.random.fold_in(rng, 6)
    for dim, parts in shards:
        draws = jnp.exp(jax.random.uniform(jax.random.fold_in(own, dim), (parts,), jnp.float32, smallest / len(shards), top_value / len(shards)))
        factor_of = factor_of * jnp.repeat(draws, shape[dim] // parts).reshape([-1 if axis == dim else 1 for axis in range(len(shape))])
    return factor_of


def gaussian(rng, shape, scale, most, pieces=(), kind=jnp.bfloat16):
    drawn = jax.random.normal(rng, shape, jnp.float32) * scale
    if len(pieces) > 0:
        drawn = block_scale(rng, shape, pieces, -0.22, 0.18) * drawn
    return jnp.clip(drawn, min=-most, max=most).astype(kind)


def noise_with(rng, dims, scale, bound, cuts, heavy, kind=jnp.bfloat16):
    drawn = scale * jax.random.normal(rng, dims, jnp.float32)
    if cuts:
        drawn = drawn * block_scale(rng, dims, cuts, -0.22, 0.18)
    return jnp.clip(raised(drawn, jax.random.fold_in(rng, 3), *heavy), -bound, bound).astype(kind)


def setup_inputs(seed: int = 0) -> dict:
    arg_keys = jax.random.split(jax.random.key(seed), 7)
    return {
        "span_act": noise_with(arg_keys[0], (TOKENS, D), 1.0, 6.0, ((0, 32), (1, 8)), (0, 1, 32, 2.75)),
        "q_weight": gaussian(arg_keys[1], (D, HW), D ** -0.5, 0.0625, ((0, 32), (1, 8))),
        "out_grad": gaussian(arg_keys[2], (TOKENS, HW), 1.0, 6.0, ((0, 32), (1, 8))),
        "neighbour_kv": draw_neighbour_kv(jax.random.fold_in(arg_keys[6], 71), 0),
        "neighbour_ids": draw_neighbour_ids(jax.random.fold_in(arg_keys[6], 71), 0),
        "owner": draw_owner(jax.random.fold_in(arg_keys[6], 71), 0),
    }


def settle(values):
    return lax.optimization_barrier(values.astype(jnp.bfloat16)).astype(jnp.float32)


def attend_back(queries, grads, pair_kv, live):
    rows, width = queries.shape
    heads = width // HD
    scale = HD ** -0.5
    query_heads = queries.astype(jnp.float32).reshape(rows, heads, HD)
    grad_heads = grads.astype(jnp.float32).reshape(rows, heads, HD)
    key_heads = pair_kv[0].astype(jnp.float32).reshape(-1, heads, HD)
    value_heads = pair_kv[1].astype(jnp.float32).reshape(-1, heads, HD)
    scores = jnp.einsum('qhd,khd->hqk', query_heads, key_heads) * scale
    scores = jnp.where(live[None, None, :], scores, -1e30)
    top = jnp.max(scores, axis=-1, keepdims=True)
    expo = jnp.exp(scores - top)
    probs = expo / jnp.sum(expo, axis=-1, keepdims=True)
    value_grad = jnp.einsum('hqk,qhd->khd', settle(probs), grad_heads)
    prob_grad = jnp.einsum('qhd,khd->hqk', grad_heads, value_heads)
    center = jnp.sum(probs * prob_grad, axis=-1, keepdims=True)
    score_grad = settle(probs * (prob_grad - center) * scale)
    query_grad = jnp.einsum('hqk,khd->qhd', score_grad, key_heads)
    key_grad = jnp.einsum('hqk,qhd->khd', score_grad, query_heads)
    both = jnp.stack([key_grad, value_grad], axis=0).reshape(2, -1, width)
    return query_grad.reshape(rows, width).astype(jnp.bfloat16), both.astype(jnp.bfloat16)


def reference(span_act, q_weight, out_grad, neighbour_kv, neighbour_ids, owner):
    queries = jnp.dot(span_act, q_weight, preferred_element_type=jnp.float32).astype(jnp.bfloat16)
    blocks = N_SEQ * N_DP
    groups = owner.reshape(blocks, CH_DEV)
    position = jnp.arange(CH_DEV)
    same = groups[:, :, None] == groups[:, None, :]
    before = position[None, :] < position[:, None]
    rank = jnp.sum(same & before[None, :, :], axis=2).astype(jnp.int32)
    block_id = jnp.arange(blocks).astype(jnp.int32)[:, None]
    slot = ((groups * N_DP + block_id % N_DP) * CAP + (block_id // N_DP) * PAIR + rank).reshape(-1).astype(jnp.int32)
    q_spans = queries.reshape(SPANS, SPAN, HW)
    g_spans = out_grad.reshape(SPANS, SPAN, HW)
    live = neighbour_ids != 0

    def one(index):
        where = slot[index]
        return attend_back(q_spans[index], g_spans[index], neighbour_kv[where], live[where])

    span_qgrad, span_kv = lax.map(one, jnp.arange(SPANS).astype(jnp.int32))
    kv_grad = jnp.zeros(neighbour_kv.shape, jnp.bfloat16).at[slot].set(span_kv)
    query_grad = span_qgrad.reshape(TOKENS, HW)
    group_width = HW // N_TENSOR
    act_total = jnp.zeros((TOKENS, D), jnp.float32)
    for group in range(N_TENSOR):
        left = query_grad[:, group * group_width:(group + 1) * group_width]
        right = q_weight[:, group * group_width:(group + 1) * group_width]
        part = lax.dot_general(left, right, (((1,), (1,)), ((), ())), preferred_element_type=jnp.float32)
        act_total = act_total + settle(part)
    act_grad = act_total.astype(jnp.bfloat16)
    weight_total = jnp.zeros((D, HW), jnp.float32)
    for index in range(blocks):
        rows_act = span_act[index * TOK_DEV:(index + 1) * TOK_DEV]
        rows_grad = query_grad[index * TOK_DEV:(index + 1) * TOK_DEV]
        part = lax.dot_general(rows_act, rows_grad, (((0,), (0,)), ((), ())), preferred_element_type=jnp.float32)
        weight_total = weight_total + settle(part)
    return act_grad, weight_total, kv_grad
```

```python
import jax
import jax.numpy as jnp
from jax import lax
from jax.sharding import PartitionSpec as P

HD = 128
SPAN = 64
KEYS = 256


def attend_back(queries, grads, pair_kv, live):
    slots, rows, width = queries.shape
    heads = width // HD
    scale = HD ** (-0.5)
    query_heads = queries.reshape(slots, rows, heads, HD)
    grad_heads = grads.reshape(slots, rows, heads, HD)
    key_heads = pair_kv[:, 0].reshape(slots, -1, heads, HD)
    value_heads = pair_kv[:, 1].reshape(slots, -1, heads, HD)
    scores = (
        jnp.einsum("bqhd,bkhd->bhqk", query_heads, key_heads, preferred_element_type=jnp.float32)
        * scale
    )
    scores = jnp.where(live[:, None, None, :], scores, -1e30)
    top = jnp.max(scores, axis=-1, keepdims=True)
    expo = jnp.exp(scores - top)
    probs = expo / jnp.sum(expo, axis=-1, keepdims=True)
    value_grad = jnp.einsum(
        "bhqk,bqhd->bkhd",
        probs.astype(jnp.bfloat16),
        grad_heads,
        preferred_element_type=jnp.float32,
    )
    prob_grad = jnp.einsum(
        "bqhd,bkhd->bhqk", grad_heads, value_heads, preferred_element_type=jnp.float32
    )
    center = jnp.sum(probs * prob_grad, axis=-1, keepdims=True)
    score_grad = (probs * (prob_grad - center) * scale).astype(jnp.bfloat16)
    query_grad = jnp.einsum(
        "bhqk,bkhd->bqhd", score_grad, key_heads, preferred_element_type=jnp.float32
    )
    key_grad = jnp.einsum(
        "bhqk,bqhd->bkhd", score_grad, query_heads, preferred_element_type=jnp.float32
    )
    both = jnp.stack([key_grad.astype(jnp.bfloat16), value_grad.astype(jnp.bfloat16)], axis=1)
    return (
        query_grad.astype(jnp.bfloat16).reshape(slots, rows, width),
        both.reshape(slots, 2, -1, width),
    )


def on_device(span_act, q_weight, out_grad, neighbour_kv, neighbour_ids, owner):
    tok_rows = out_grad.shape[0]
    width = out_grad.shape[1]
    seq_count = lax.axis_size("seq")
    dp_count = lax.axis_size("dp")
    spans_dev = tok_rows // SPAN
    capacity = neighbour_kv.shape[0]
    pairs = capacity // seq_count
    block = lax.axis_index("seq") * dp_count + lax.axis_index("dp")
    whole = lax.all_gather(span_act, "tensor", axis=1, tiled=True)
    weights = lax.all_gather(q_weight, ("seq", "dp"), axis=0, tiled=True)
    queries = jnp.dot(whole, weights, preferred_element_type=jnp.float32).astype(jnp.bfloat16)
    mine = lax.dynamic_slice_in_dim(owner, block * spans_dev, spans_dev)
    position = jnp.arange(spans_dev)
    same = mine[:, None] == mine[None, :]
    before = position[None, :] < position[:, None]
    rank = jnp.sum(same & before, axis=1)
    target = mine * pairs + rank
    select = jnp.arange(capacity)[:, None] == target[None, :]

    def to_owner(rows):
        spans = rows.reshape(spans_dev, SPAN, width)
        slots = jnp.zeros((capacity, SPAN, width), rows.dtype)
        for c in range(spans_dev):
            slots = jnp.where(select[:, c][:, None, None], spans[c][None], slots)
        return lax.all_to_all(
            slots.reshape(seq_count, pairs, SPAN, width),
            "seq",
            split_axis=0,
            concat_axis=0,
            tiled=True,
        ).reshape(capacity, SPAN, width)

    g_slots = to_owner(out_grad)
    q_slots = to_owner(queries)
    slot_grad, kv_grad = attend_back(q_slots, g_slots, neighbour_kv, neighbour_ids != 0)
    home_grad = lax.all_to_all(
        slot_grad.reshape(seq_count, pairs, SPAN, width),
        "seq",
        split_axis=0,
        concat_axis=0,
        tiled=True,
    ).reshape(capacity, SPAN, width)
    query_grad = jnp.zeros((spans_dev, SPAN, width), home_grad.dtype)
    for s in range(capacity):
        query_grad = jnp.where(select[s][:, None, None], home_grad[s][None], query_grad)
    flat_grad = query_grad.reshape(tok_rows, width)
    partial_act = lax.dot_general(
        flat_grad, weights, (((1,), (1,)), ((), ())), preferred_element_type=jnp.float32
    )
    act_grad = lax.psum_scatter(
        partial_act.astype(jnp.bfloat16), "tensor", scatter_dimension=1, tiled=True
    )
    weight_grad = lax.psum_scatter(
        lax.dot_general(
            whole, flat_grad, (((0,), (0,)), ((), ())), preferred_element_type=jnp.float32
        ).astype(jnp.bfloat16),
        ("seq", "dp"),
        scatter_dimension=0,
        tiled=True,
    ).astype(jnp.float32)
    return (act_grad, weight_grad, kv_grad)


def solution(mesh):
    in_specs = (
        P(("seq", "dp"), "tensor"),
        P(("seq", "dp"), "tensor"),
        P(("seq", "dp"), "tensor"),
        P(("seq", "dp"), None, None, "tensor"),
        P(("seq", "dp"), None),
        P(),
    )
    out_specs = (
        P(("seq", "dp"), "tensor"),
        P(("seq", "dp"), "tensor"),
        P(("seq", "dp"), None, None, "tensor"),
    )
    return jax.shard_map(
        on_device, mesh=mesh, in_specs=in_specs, out_specs=out_specs, check_vma=False
    )
```

```python
import functools

import jax
import jax.numpy as jnp
from jax import lax
from jax.experimental import pallas as pl
from jax.experimental.pallas import tpu as pltpu
from jax.sharding import PartitionSpec as P

HD = 128
SPAN = 64
KEYS = 256
MESH = pl.DeviceIdType.MESH
BF = jnp.bfloat16
F32 = jnp.float32
NN = (((1,), (0,)), ((), ()))
NT = (((1,), (1,)), ((), ()))
TN = (((0,), (0,)), ((), ()))


def dot(a, b, dims):
    return lax.dot_general(a, b, dims, preferred_element_type=F32)


def kernel(
    act_ref, w_ref, g_ref, kv_ref, ids_ref, owner_ref,
    act_out, w_out, kv_out,
    act_full, act_t, w_full, kv_v, kvg, g_v, q_acc,
    q_send, q_recv, g_send, g_recv, dq_send, dq_recv, dq_v,
    z_send, z_recv, sib_send, red, p1q, p1h, s1h, f1, f1b, s2h, p2q, p2h,
    send_sems, recv_sems, dq_ssem, dq_rsem, loc_sems, kv_sems,
):
    s = lax.axis_index("seq")
    z = lax.axis_index("tensor")
    y = lax.axis_index("dp")
    x = s // 2
    core = s % 2
    TOK = g_v.shape[0]
    HALF = TOK // 2
    QUART = HALF // 2
    BLK = w_ref.shape[0]

    def mod4(v):
        return lax.rem(v + 4, 4)

    def mod8(v):
        return lax.rem(v + 8, 8)

    z_dev = {1: {"tensor": mod8(z + 1)}, -1: {"tensor": mod8(z - 1)}}
    x_dev = {1: {"seq": mod4(x + 1) * 2 + core}, -1: {"seq": mod4(x - 1) * 2 + core}}
    y_dev = {1: {"dp": mod4(y + 1)}, -1: {"dp": mod4(y - 1)}}
    sib = {"seq": s + 1 - 2 * core}

    barrier = pltpu.get_barrier_semaphore()
    partners = [z_dev[1], z_dev[-1], y_dev[1], y_dev[-1]]
    partners += [{"seq": mod8(s + k)} for k in range(1, 8)]
    for dev in partners:
        pl.semaphore_signal(barrier, inc=1, device_id=dev, device_id_type=MESH)

    loads = []

    def load(src, dst):
        d = pltpu.make_async_copy(src, dst, loc_sems.at[len(loads)])
        d.start()
        loads.append(d)
        return d

    own_rows = pl.ds(pl.multiple_of(y * BLK, BLK), BLK)
    ld_act = load(act_ref, act_full.at[z])
    ld_w = load(w_ref, w_full.at[s, own_rows])
    ld_g = load(g_ref, g_v)
    ld_kv = load(kv_ref, kv_v)
    pl.semaphore_wait(barrier, len(partners))

    sends = []

    def push(src, dst, dev):
        n = len(sends)
        d = pltpu.make_async_remote_copy(
            src_ref=src, dst_ref=dst, send_sem=send_sems.at[n], recv_sem=recv_sems.at[n],
            device_id=dev, device_id_type=MESH,
        )
        d.start()
        sends.append(d)
        return d

    def act_rows(chunk):
        return pl.ds(chunk * HALF, HALF)

    zf = {}

    def z_first(chunk):
        for d in (1, -1):
            zf[d, 0, chunk] = push(
                act_ref.at[act_rows(chunk)], act_full.at[z, act_rows(chunk)], z_dev[d]
            )

    def z_fwd(t, chunk):
        for d in (1, -1):
            if (d, t, chunk) not in zf:
                continue
            zf[d, t, chunk].wait_recv()
            last = t == 3 or (t == 2 and chunk != (0 if d == 1 else 1))
            if not last:
                ref = act_full.at[mod8(z - d * (t + 1)), act_rows(chunk)]
                zf[d, t + 1, chunk] = push(ref, ref, z_dev[d])

    def w_ref_at(h, k1, k2, off, n, c=None):
        dx, dy = (k1, k2) if h == 0 else (k2, k1)
        seq = mod4(x + dx) * 2 + (core if c is None else c)
        return w_full.at[seq, pl.ds(pl.multiple_of(mod4(y + dy) * BLK + h * HALF + off, QUART), n)]

    ax = {0: (x_dev, y_dev), 1: (y_dev, x_dev)}
    sib_w = []

    def to_sib(h, k1, k2):
        ref = w_ref_at(h, k1, k2, 0, HALF)
        sib_w.append(push(ref, ref, sib))

    wp1, wp1b, wp2, wp2b = {}, {}, {}, {}

    def w_start_p1(h):
        src = w_ref.at[pl.ds(h * HALF, HALF)]
        for d in (1, -1):
            wp1[h, d] = push(src, w_ref_at(h, 0, 0, 0, HALF), ax[h][0][d])

    def w_start_p2(h):
        src = w_ref.at[pl.ds(h * HALF, HALF)]
        for d in (1, -1):
            wp2[h, 0, d] = push(src, w_ref_at(h, 0, 0, 0, HALF), ax[h][1][d])

    def w_p2_send(h, k):
        ref = w_ref_at(h, k, 0, 0, HALF)
        for d in (1, -1):
            wp2[h, k, d] = push(ref, ref, ax[h][1][d])

    def w_p1_hop1(h):
        for d in (1, -1):
            wp1[h, d].wait_recv()
            ref = w_ref_at(h, -d, 0, 0 if d == 1 else QUART, QUART)
            wp1b[h, d] = push(ref, ref, ax[h][0][d])
            w_p2_send(h, -d)
            to_sib(h, -d, 0)

    def w_p1_hop2(h):
        for d in (1, -1):
            wp1b[h, d].wait_recv()
        w_p2_send(h, 2)
        to_sib(h, 2, 0)

    def w_p2_hop1(h, k):
        for d in (1, -1):
            wp2[h, k, d].wait_recv()
            ref = w_ref_at(h, k, -d, 0 if d == 1 else QUART, QUART)
            wp2b[h, k, d] = push(ref, ref, ax[h][1][d])
            to_sib(h, k, -d)

    def w_p2_hop2(h, k):
        for d in (1, -1):
            wp2b[h, k, d].wait_recv()
        to_sib(h, k, 2)

    both = (0, 1)
    z_first(0)
    for h in both:
        w_start_p1(h)
    for h in both:
        w_start_p2(h)
    z_first(1)
    sib_w.append(push(w_ref, w_full.at[s, own_rows], sib))

    block = s * 4 + y
    names = [owner_ref[block * 4 + c] for c in range(4)]

    def to_slots(rows_ref, send, recv):
        for k in range(8):
            o = mod8(s + k)
            v = jnp.zeros((SPAN, rows_ref.shape[1]), BF)
            for c in range(4):
                v = jnp.where(names[c] == o, rows_ref[c * SPAN:(c + 1) * SPAN, :].astype(BF), v)
            if k == 0:
                recv[s] = v
            else:
                send[k] = v

    ld_g.wait()
    to_slots(g_v, g_send, g_recv)
    ld_act.wait()
    ld_w.wait()

    for h in both:
        w_p1_hop1(h)
    z_fwd(0, 0)
    for h in both:
        w_p2_hop1(h, 0)
    for h in both:
        w_p1_hop2(h)
    g_copies = {
        k: push(g_send.at[k], g_recv.at[s], {"seq": mod8(s + k)}) for k in range(1, 8)
    }
    z_fwd(0, 1)

    def turn(slot):
        act_t[slot] = jnp.transpose(act_full[slot])

    turn(z)
    for h in both:
        w_p2_hop1(h, -1)
        w_p2_hop1(h, 1)
    z_fwd(1, 0)
    for h in both:
        w_p2_hop1(h, 2)
    z_fwd(1, 1)
    for h in both:
        w_p2_hop2(h, 0)
    turn(mod8(z + 1))
    turn(mod8(z - 1))
    for h in both:
        w_p2_hop2(h, -1)
        w_p2_hop2(h, 1)
    z_fwd(2, 0)
    for h in both:
        w_p2_hop2(h, 2)
    for d in sib_w:
        d.wait_recv()

    def add_q(slot):
        q_acc[...] += dot(act_full[slot], w_full[slot], NN)

    q_acc[...] = jnp.zeros_like(q_acc)
    add_q(z)
    for k in (1, -1):
        add_q(mod8(z + k))
    z_fwd(2, 1)
    for k in (2, -2):
        add_q(mod8(z + k))
        turn(mod8(z + k))
    for k in (3, -3):
        add_q(mod8(z + k))
        turn(mod8(z + k))
    ld_kv.wait()
    z_fwd(3, 0)
    z_fwd(3, 1)
    add_q(mod8(z + 4))

    to_slots(q_acc, q_send, q_recv)
    q_copies = {
        k: push(q_send.at[k], q_recv.at[s], {"seq": mod8(s + k)}) for k in range(1, 8)
    }
    turn(mod8(z + 4))
    for k in range(1, 8):
        g_copies[k].wait_recv()
    for k in range(1, 8):
        q_copies[k].wait_recv()
    scale = HD ** (-0.5)
    heads = g_v.shape[1] // HD

    def dq_copy(k):
        j = mod8(s - k)
        return pltpu.make_async_remote_copy(
            src_ref=dq_send.at[j], dst_ref=dq_recv.at[s], send_sem=dq_ssem.at[k],
            recv_sem=dq_rsem.at[k], device_id={"seq": j}, device_id_type=MESH,
        )

    def kv_copy(k):
        j = mod8(s - k)
        return pltpu.make_async_copy(kvg.at[j], kv_out.at[j], kv_sems.at[k])

    def slot_step(i, carry):
        k = 7 - i
        j = mod8(s - k)
        live = ids_ref[pl.ds(j, 1), :] != 0
        for h in range(heads):
            cols = slice(h * HD, (h + 1) * HD)
            q = q_recv[j, :, cols]
            g = g_recv[j, :, cols]
            key = kv_v[j, 0, :, cols]
            val = kv_v[j, 1, :, cols]
            sc = jnp.where(live, dot(q, key, NT) * scale, -1e30)
            ex = jnp.exp(sc - jnp.max(sc, axis=1, keepdims=True))
            probs = ex / jnp.sum(ex, axis=1, keepdims=True)
            pg = dot(g, val, NT)
            center = jnp.sum(probs * pg, axis=1, keepdims=True)
            sg = (probs * (pg - center) * scale).astype(BF)
            dq_send[j, :, cols] = dot(sg, key, NN).astype(BF)
            kvg[j, 0, :, cols] = dot(sg, q, TN).astype(BF)
            kvg[j, 1, :, cols] = dot(probs.astype(BF), g, TN).astype(BF)

        @pl.when(k > 0)
        def _():
            dq_copy(k).start()

        kv_copy(k).start()
        return carry

    lax.fori_loop(0, 8, slot_step, 0)
    dq_recv[s] = dq_send[s]
    for k in range(1, 8):
        dq_copy(k).wait_recv()
    for c in range(4):
        v = jnp.zeros((SPAN, g_v.shape[1]), BF)
        for o in range(8):
            v = jnp.where(names[c] == o, dq_recv[o], v)
        dq_v[c * SPAN:(c + 1) * SPAN, :] = v

    def part_act(dest, chunk):
        return dot(dq_v[chunk * HALF:(chunk + 1) * HALF, :], w_full[mod8(dest)], NT)

    zb = {}

    def z_push(d, dist, chunk, value):
        n = len(zb)
        z_send[n] = value.astype(BF)
        zb[d, dist, chunk] = (push(z_send.at[n], z_recv.at[n], z_dev[d]), n)

    def z_got(d, dist, chunk):
        copy, n = zb[d, dist, chunk]
        copy.wait_recv()
        return z_recv[n].astype(F32)

    def z_add(dist, chunk):
        for d in (1, -1):
            ch = chunk if d == 1 else 1 - chunk
            got = z_got(d, dist, ch)
            z_push(d, dist - 1, ch, got + part_act(z + d * (dist - 1), ch))

    z_push(1, 4, 0, part_act(z + 4, 0))
    z_push(-1, 4, 1, part_act(z + 4, 1))
    z_push(1, 3, 1, part_act(z + 3, 1))
    z_push(-1, 3, 0, part_act(z - 3, 0))

    order = [(kx, 2) for kx in (2, 1, 3, 0)] + [(2, ky) for ky in (1, 3, 0)]
    order += [(kx, ky) for kx in (1, 3, 0) for ky in (1, 3, 0)]

    def part_w(kx, ky, c):
        rows = pl.ds(pl.multiple_of(mod4(y + ky) * BLK, BLK), BLK)
        return dot(act_t[mod4(x + kx) * 2 + c, rows], dq_v[...], NN)

    sib_d = {}
    for n, (kx, ky) in enumerate(order):
        sib_send[n] = part_w(kx, ky, 1 - core).astype(BF)
        sib_d[kx, ky] = (push(sib_send.at[n], red.at[n], sib), n)
    z_add(4, 0)

    def red_at(h, kf, ku, off, n):
        kx, ky = (kf, ku) if h == 0 else (ku, kf)
        return red.at[order.index((kx % 4, ky % 4)), pl.ds(h * HALF + off, n)]

    def pair_sum(kx, ky):
        copy, n = sib_d[kx, ky]
        copy.wait_recv()
        red[n] = (red[n].astype(F32) + part_w(kx, ky, core)).astype(BF)

    first_ax = {0: y_dev, 1: x_dev}
    second_ax = {0: x_dev, 1: y_dev}
    c1q, c1h, c2q, c2h = {}, {}, {}, {}

    def quarter1(h, kf):
        c1q[h, 1, kf] = push(red_at(h, kf, 2, 0, QUART), p1q.at[h, 0, kf], first_ax[h][1])
        c1q[h, -1, kf] = push(red_at(h, kf, 2, QUART, QUART), p1q.at[h, 1, kf], first_ax[h][-1])

    def half1(h, kf):
        for e, d in enumerate((1, -1)):
            c1q[h, d, kf].wait_recv()
            src = red_at(h, kf, d, 0, HALF)
            got = p1q[h, e, kf].astype(F32)
            lo = src[:QUART].astype(F32)
            hi = src[QUART:].astype(F32)
            lo, hi = (lo + got, hi) if d == 1 else (lo, hi + got)
            s1h[h, e, kf, :QUART] = lo.astype(BF)
            s1h[h, e, kf, QUART:] = hi.astype(BF)
            c1h[h, d, kf] = push(s1h.at[h, e, kf], p1h.at[h, e, kf], first_ax[h][d])

    def final1(h, kf):
        for d in (1, -1):
            c1h[h, d, kf].wait_recv()
        v = red_at(h, kf, 0, 0, HALF)[...].astype(F32)
        v = v + p1h[h, 0, kf].astype(F32) + p1h[h, 1, kf].astype(F32)
        if kf == 2:
            f1b[h] = v.astype(BF)
            c2q[h, 1] = push(f1b.at[h, pl.ds(0, QUART)], p2q.at[h, 0], second_ax[h][1])
            c2q[h, -1] = push(f1b.at[h, pl.ds(QUART, QUART)], p2q.at[h, 1], second_ax[h][-1])
        else:
            f1[h, kf] = v

    def half2(h):
        for e, d in enumerate((1, -1)):
            c2q[h, d].wait_recv()
            got = p2q[h, e].astype(F32)
            lo = f1[h, d % 4, :QUART]
            hi = f1[h, d % 4, QUART:]
            lo, hi = (lo + got, hi) if d == 1 else (lo, hi + got)
            s2h[h, e, :QUART] = lo.astype(BF)
            s2h[h, e, QUART:] = hi.astype(BF)
            c2h[h, d] = push(s2h.at[h, e], p2h.at[h, e], second_ax[h][d])

    def final2(h):
        for d in (1, -1):
            c2h[h, d].wait_recv()
        w_out[h * HALF:(h + 1) * HALF, :] = (
            f1[h, 0] + p2h[h, 0].astype(F32) + p2h[h, 1].astype(F32)
        )

    for kx, ky in order[:4]:
        pair_sum(kx, ky)
        quarter1(0, kx)
    for ky in (2, 1, 3, 0):
        if ky != 2:
            pair_sum(2, ky)
        quarter1(1, ky)
    z_add(3, 1)
    for kx, ky in order[7:]:
        pair_sum(kx, ky)
    for kf in (2, 1, 3, 0):
        for h in both:
            half1(h, kf)
    z_add(3, 0)
    for h in both:
        final1(h, 2)
    z_add(2, 1)
    for kf in (1, 3):
        for h in both:
            final1(h, kf)
    for h in both:
        half2(h)
    for h in both:
        final1(h, 0)
    z_add(2, 0)
    for h in both:
        final2(h)
    for chunk in (1, 0):
        own = part_act(z, chunk)
        got = z_got(1, 1, chunk) + z_got(-1, 1, chunk)
        act_out[chunk * HALF:(chunk + 1) * HALF, :] = (own + got).astype(BF)

    for d in sends:
        d.wait_send()
    for k in range(8):
        if k:
            dq_copy(k).wait_send()
        kv_copy(k).wait()


def on_device(span_act, q_weight, out_grad, neighbour_kv, neighbour_ids, owner):
    tok, width = out_grad.shape
    dcol = span_act.shape[1]
    half, quart = tok // 2, tok // 4
    any_spec = pl.BlockSpec(memory_space=pl.ANY)
    vmem = pl.BlockSpec(memory_space=pltpu.VMEM)

    def bf(*shape):
        return pltpu.VMEM(shape, BF)

    def f32(*shape):
        return pltpu.VMEM(shape, F32)

    return pl.pallas_call(
        kernel,
        out_shape=(
            jax.ShapeDtypeStruct((tok, dcol), BF),
            jax.ShapeDtypeStruct((q_weight.shape[0], width), F32),
            jax.ShapeDtypeStruct(neighbour_kv.shape, BF),
        ),
        in_specs=[any_spec, any_spec, any_spec, any_spec, vmem,
                  pl.BlockSpec(memory_space=pltpu.SMEM)],
        out_specs=(vmem, vmem, any_spec),
        scratch_shapes=[
            bf(8, tok, dcol), bf(8, dcol, tok), bf(8, dcol, width),
            bf(*neighbour_kv.shape), bf(*neighbour_kv.shape), bf(tok, width), f32(tok, width),
            bf(8, SPAN, width), bf(8, SPAN, width), bf(8, SPAN, width), bf(8, SPAN, width),
            bf(8, SPAN, width), bf(8, SPAN, width), bf(tok, width),
            bf(14, half, dcol), bf(14, half, dcol),
            bf(16, tok, width), bf(16, tok, width),
            bf(2, 2, 4, quart, width), bf(2, 2, 4, half, width), bf(2, 2, 4, half, width),
            f32(2, 4, half, width), bf(2, half, width), bf(2, 2, half, width),
            bf(2, 2, quart, width), bf(2, 2, half, width),
            pltpu.SemaphoreType.DMA((180,)), pltpu.SemaphoreType.DMA((180,)),
            pltpu.SemaphoreType.DMA((8,)), pltpu.SemaphoreType.DMA((8,)),
            pltpu.SemaphoreType.DMA((4,)), pltpu.SemaphoreType.DMA((8,)),
        ],
        compiler_params=pltpu.CompilerParams(
            collective_id=0, has_side_effects=True, vmem_limit_bytes=60 * 1024 * 1024
        ),
        cost_estimate=pl.CostEstimate(
            flops=8 * 10**9, bytes_accessed=16 * 2**20, transcendentals=600000
        ),
    )(span_act, q_weight, out_grad, neighbour_kv, neighbour_ids, owner)


def solution(mesh):
    in_specs = (
        P(("seq", "dp"), "tensor"),
        P(("seq", "dp"), "tensor"),
        P(("seq", "dp"), "tensor"),
        P(("seq", "dp"), None, None, "tensor"),
        P(("seq", "dp"), None),
        P(),
    )
    out_specs = (
        P(("seq", "dp"), "tensor"),
        P(("seq", "dp"), "tensor"),
        P(("seq", "dp"), None, None, "tensor"),
    )
    return jax.shard_map(
        on_device, mesh=mesh, in_specs=in_specs, out_specs=out_specs, check_vma=False
    )
```

```python
import functools

import jax
import jax.numpy as jnp
from jax import lax
from jax.experimental import pallas as pl
from jax.experimental.pallas import tpu as pltpu
from jax.sharding import PartitionSpec as P

HD = 128
SPAN = 64
KEYS = 256
MESH = pl.DeviceIdType.MESH
BF = jnp.bfloat16
F32 = jnp.float32
NN = (((1,), (0,)), ((), ()))
NT = (((1,), (1,)), ((), ()))
TN = (((0,), (0,)), ((), ()))


def dot(a, b, dims):
    return lax.dot_general(a, b, dims, preferred_element_type=F32)


def kernel(
    act_ref, w_ref, g_ref, kv_ref, ids_ref, owner_ref,
    act_o, w_o, kv_out,
    act_out, w_out,
    act_full, act_t, w_full, kv_v, pg_v, probs_v, sg_v, g_v, q_acc, q_v,
    q_send, q_recv, g_send, g_recv, dq_send, dq_recv, dq_v,
    z_send, z_recv, pend, sib_send, red, p1q, p1h, s1h, f1, f1b, s2h, p2q, p2h,
    send_sems, recv_sems, g_ssem, g_rsem, q_ssem, q_rsem, dq_ssem, dq_rsem, loc_sems, kv_sems, out_sems,
):
    s = lax.axis_index("seq")
    z = lax.axis_index("tensor")
    y = lax.axis_index("dp")
    x = s // 2
    core = s % 2
    TOK = g_v.shape[0]
    HALF = TOK // 2
    QUART = HALF // 2
    BLK = w_ref.shape[0]

    def mod4(v):
        return lax.rem(v + 4, 4)

    def mod8(v):
        return lax.rem(v + 8, 8)

    z_dev = {1: {"tensor": mod8(z + 1)}, -1: {"tensor": mod8(z - 1)}}
    x_dev = {1: {"seq": mod4(x + 1) * 2 + core}, -1: {"seq": mod4(x - 1) * 2 + core}}
    y_dev = {1: {"dp": mod4(y + 1)}, -1: {"dp": mod4(y - 1)}}
    sib = {"seq": s + 1 - 2 * core}

    barrier = pltpu.get_barrier_semaphore()
    partners = [z_dev[1], z_dev[-1], y_dev[1], y_dev[-1]]
    partners += [{"seq": mod8(s + k)} for k in range(1, 8)]
    for dev in partners:
        pl.semaphore_signal(barrier, inc=1, device_id=dev, device_id_type=MESH)

    loads = []

    def load(src, dst):
        d = pltpu.make_async_copy(src, dst, loc_sems.at[len(loads)])
        d.start()
        loads.append(d)
        return d

    own_rows = pl.ds(pl.multiple_of(y * BLK, BLK), BLK)
    PART = SPAN // 2
    ld_act = [
        load(
            act_ref.at[pl.ds(c * SPAN + ch * PART, PART)],
            act_full.at[z, pl.ds(ch * HALF + c * PART, PART)],
        )
        for ch in (0, 1) for c in range(4)
    ]
    ld_w = load(w_ref, w_full.at[s, own_rows])
    ld_g = load(g_ref, g_v)
    ld_kv = load(kv_ref, kv_v)
    pl.semaphore_wait(barrier, len(partners))

    sends = []
    used = []

    def push(src, dst, dev):
        n = len(used)
        used.append(n)
        d = pltpu.make_async_remote_copy(
            src_ref=src, dst_ref=dst, send_sem=send_sems.at[n], recv_sem=recv_sems.at[n],
            device_id=dev, device_id_type=MESH,
        )
        d.start()
        sends.append(d)
        return d

    def act_rows(ch, sub):
        return pl.ds(ch * HALF + sub * QUART, QUART)

    zf = {}

    def z_first(ch):
        for sub in (0, 1):
            if ch == 0:
                for d in (1, -1):
                    zf[d, 0, ch, sub] = [
                        push(
                            act_ref.at[pl.ds(c * SPAN, PART)],
                            act_full.at[z, pl.ds(c * PART, PART)], z_dev[d],
                        )
                        for c in (2 * sub, 2 * sub + 1)
                    ]
            else:
                ref = act_full.at[z, act_rows(ch, sub)]
                for d in (1, -1):
                    zf[d, 0, ch, sub] = [push(ref, ref, z_dev[d])]

    def z_fwd(ch, t, sub):
        for d in (1, -1):
            if (d, t, ch, sub) not in zf:
                continue
            for copy in zf[d, t, ch, sub]:
                copy.wait_recv()
            if t < 2 or (t == 2 and sub == (0 if d == 1 else 1)):
                ref = act_full.at[mod8(z - d * (t + 1)), act_rows(ch, sub)]
                zf[d, t + 1, ch, sub] = [push(ref, ref, z_dev[d])]

    def w_ref_at(h, k1, k2, off, n, c=None):
        dx, dy = (k1, k2) if h == 0 else (k2, k1)
        seq = mod4(x + dx) * 2 + (core if c is None else c)
        return w_full.at[seq, pl.ds(pl.multiple_of(mod4(y + dy) * BLK + h * HALF + off, QUART), n)]

    ax = {0: (x_dev, y_dev), 1: (y_dev, x_dev)}
    sib_w = []

    def to_sib(h, k1, k2):
        ref = w_ref_at(h, k1, k2, 0, HALF)
        sib_w.append(push(ref, ref, sib))

    wp1, wp1b, wp2, wp2b = {}, {}, {}, {}

    def w_start_p1(h):
        src = w_ref.at[pl.ds(h * HALF, HALF)]
        for d in (1, -1):
            wp1[h, d] = push(src, w_ref_at(h, 0, 0, 0, HALF), ax[h][0][d])

    def w_start_p2(h):
        src = w_ref.at[pl.ds(h * HALF, HALF)]
        for d in (1, -1):
            wp2[h, 0, d] = push(src, w_ref_at(h, 0, 0, 0, HALF), ax[h][1][d])

    def w_p2_send(h, k):
        ref = w_ref_at(h, k, 0, 0, HALF)
        for d in (1, -1):
            wp2[h, k, d] = push(ref, ref, ax[h][1][d])

    def w_p1_hop1(h):
        for d in (1, -1):
            wp1[h, d].wait_recv()
            ref = w_ref_at(h, -d, 0, 0 if d == 1 else QUART, QUART)
            wp1b[h, d] = push(ref, ref, ax[h][0][d])
            w_p2_send(h, -d)
            to_sib(h, -d, 0)

    def w_p1_hop2(h):
        for d in (1, -1):
            wp1b[h, d].wait_recv()
        w_p2_send(h, 2)
        to_sib(h, 2, 0)

    def w_p2_hop1(h, k):
        for d in (1, -1):
            wp2[h, k, d].wait_recv()
            ref = w_ref_at(h, k, -d, 0 if d == 1 else QUART, QUART)
            wp2b[h, k, d] = push(ref, ref, ax[h][1][d])
            to_sib(h, k, -d)

    def w_p2_hop2(h, k):
        for d in (1, -1):
            wp2b[h, k, d].wait_recv()
        to_sib(h, k, 2)

    both = (0, 1)
    z_first(0)
    for h in both:
        w_start_p1(h)
    for h in both:
        w_start_p2(h)
    for d in ld_act:
        d.wait()
    z_first(1)
    sib_w.append(push(w_ref, w_full.at[s, own_rows], sib))

    block = s * 4 + y
    names = [owner_ref[block * 4 + c] for c in range(4)]

    def peer(dx, dc):
        return mod4(x + dx) * 2 + lax.rem(core + dc, 2)

    def owner_copy(send, recv, ssem, rsem, k, dev):
        return pltpu.make_async_remote_copy(
            src_ref=send, dst_ref=recv, send_sem=ssem.at[k], recv_sem=rsem.at[k],
            device_id={"seq": dev}, device_id_type=MESH,
        )

    def picked(rows, o):
        v = jnp.zeros(rows[0].shape, BF)
        for c in range(4):
            v = jnp.where(names[c] == o, rows[c], v)
        return v

    def g_pick():
        rows = [g_v[c * SPAN:(c + 1) * SPAN, :] for c in range(4)]
        for dx in range(4):
            for dc in (0, 1):
                o, k = peer(dx, dc), dx * 2 + dc
                if k == 0:
                    g_recv[s] = picked(rows, o)
                else:
                    g_send[k] = picked(rows, o)

    def g_out():
        copies = {}
        for k in (4, 5, 2, 3, 6, 7, 1):
            o = peer(k // 2, k % 2)
            copies[k] = owner_copy(g_send.at[k], g_recv.at[s], g_ssem, g_rsem, k, o)
            copies[k].start()
            sends.append(copies[k])
        return copies

    def q_out(ch):
        rows = [
            q_acc[ch * HALF + c * PART:ch * HALF + (c + 1) * PART, :].astype(BF) for c in range(4)
        ]
        for dx in (2, 1, 3, 0):
            for dc in (0, 1):
                o, k = peer(dx, dc), dx * 2 + dc
                if k == 0:
                    q_recv[s, ch * PART:(ch + 1) * PART, :] = picked(rows, o)
                else:
                    q_send[ch, k] = picked(rows, o)
                    copy = owner_copy(
                        q_send.at[ch, k], q_recv.at[s, pl.ds(ch * PART, PART)],
                        q_ssem.at[ch], q_rsem.at[ch], k, o,
                    )
                    copy.start()
                    sends.append(copy)

    def turn(slot):
        act_t[slot] = jnp.transpose(act_full[slot])

    def add_q(ch, slot):
        rows = pl.ds(ch * HALF, HALF)
        q_acc[rows, :] += dot(act_full[slot, rows], w_full[slot], NN)

    scale = HD ** (-0.5)
    heads = g_v.shape[1] // HD

    def slot_of(i):
        dx = i // 2
        dx = jnp.where(dx == 2, 3, jnp.where(dx == 3, 2, dx))
        dc = lax.rem(i, 2)
        return dx * 2 + dc, mod4(x - dx) * 2 + lax.rem(core + dc, 2)

    def dq_copy(ch, k, j):
        rows = pl.ds(ch * PART, PART)
        return owner_copy(
            dq_send.at[j, rows], dq_recv.at[s, rows], dq_ssem.at[ch], dq_rsem.at[ch], k, j
        )

    def stacked(parts):
        return jnp.concatenate(parts, axis=0)

    def col(h):
        return slice(h * HD, (h + 1) * HD)

    def pg_step(j, carry):
        for h in range(heads):
            v = dot(g_recv[j, :, col(h)], kv_v[j, 1, :, col(h)], NT)
            for ch in both:
                pg_v[j, ch, h * PART:(h + 1) * PART, :] = v[ch * PART:(ch + 1) * PART, :]
        return carry

    def attend_one(ch, j):
        rows = slice(ch * PART, (ch + 1) * PART)
        live = ids_ref[pl.ds(j, 1), :] != 0
        sc = stacked(
            [dot(q_recv[j, rows, col(h)], kv_v[j, 0, :, col(h)], NT) for h in range(heads)]
        )
        sc = jnp.where(live, sc * scale, -1e30)
        ex = jnp.exp(sc - jnp.max(sc, axis=1, keepdims=True))
        probs = ex / jnp.sum(ex, axis=1, keepdims=True)
        pg = pg_v[j, ch]
        center = jnp.sum(probs * pg, axis=1, keepdims=True)
        sg = (probs * (pg - center) * scale).astype(BF)
        low = probs.astype(BF)
        for h in range(heads):
            part = slice(h * PART, (h + 1) * PART)
            dq_send[j, rows, col(h)] = dot(sg[part], kv_v[j, 0, :, col(h)], NN).astype(BF)
            probs_v[j, h, rows, :] = low[part]
            sg_v[j, h, rows, :] = sg[part]

    def attend(ch, first, last):
        def chip_step(i, carry):
            k0, j0 = slot_of(2 * i)
            k1, j1 = slot_of(2 * i + 1)

            def wait(k):
                owner_copy(
                    q_send.at[ch, k], q_recv.at[s, pl.ds(ch * PART, PART)],
                    q_ssem.at[ch], q_rsem.at[ch], k, sib["seq"],
                ).wait_recv()

            @pl.when(i > 0)
            def _():
                wait(k0)

            wait(k1)
            attend_one(ch, j0)
            attend_one(ch, j1)

            @pl.when(i > 0)
            def _():
                dq_copy(ch, k0, j0).start()

            dq_copy(ch, k1, j1).start()
            return carry

        lax.fori_loop(first, last, chip_step, 0)

    def dq_in(ch):
        mine = slice(ch * PART, (ch + 1) * PART)
        dq_recv[s, mine, :] = dq_send[s, mine, :]
        for k in range(1, 8):
            dq_copy(ch, k, sib["seq"]).wait_recv()
        for c in range(4):
            v = jnp.zeros((PART, g_v.shape[1]), BF)
            for o in range(8):
                v = jnp.where(names[c] == o, dq_recv[o, ch * PART:(ch + 1) * PART, :], v)
            dq_v[ch * HALF + c * PART:ch * HALF + (c + 1) * PART, :] = v

    def kv_copy(j):
        return pltpu.make_async_copy(kv_v.at[j], kv_out.at[j], kv_sems.at[j])

    def kv_step(j, carry):
        for h in range(heads):
            cols = slice(h * HD, (h + 1) * HD)
            kv_v[j, 0, :, cols] = dot(sg_v[j, h], q_recv[j, :, cols], TN).astype(BF)
            kv_v[j, 1, :, cols] = dot(probs_v[j, h], g_recv[j, :, cols], TN).astype(BF)
        kv_copy(j).start()
        return carry

    def part_act(dest, ch):
        return dot(dq_v[ch * HALF:(ch + 1) * HALF, :], w_full[mod8(dest)], NT)

    def sub_of(value, sub):
        return value[sub * QUART:(sub + 1) * QUART, :]

    zb = {}

    def z_push(ch, d, dist, sub, value):
        n = len(zb)
        z_send[n] = value.astype(BF)
        zb[ch, d, dist, sub] = (push(z_send.at[n], z_recv.at[n], z_dev[d]), n)

    def z_got(ch, d, dist, sub):
        copy, n = zb[ch, d, dist, sub]
        copy.wait_recv()
        return z_recv[n].astype(F32)

    def z_start(ch):
        v = part_act(z + 4, ch)
        z_push(ch, 1, 4, 0, sub_of(v, 0))
        z_push(ch, -1, 4, 1, sub_of(v, 1))
        for e, d in enumerate((1, -1)):
            v = part_act(z + 3 * d, ch)
            z_push(ch, d, 3, 1 - e, sub_of(v, 1 - e))
            pend[ch, e, 0] = sub_of(v, e)

    def z_add(ch, dist, sub):
        for e, d in enumerate((1, -1)):
            sb = sub if d == 1 else 1 - sub
            if sub == 1:
                v = part_act(z + d * (dist - 1), ch)
                pend[ch, e, 1] = sub_of(v, sb)
                pend[ch, e, 0] = sub_of(v, 1 - sb)
            z_push(ch, d, dist - 1, sb, z_got(ch, d, dist, sb) + pend[ch, e, sub])

    def z_end(ch):
        own = part_act(z, ch)
        for sub in (1, 0):
            v = sub_of(own, sub) + z_got(ch, 1, 1, sub) + z_got(ch, -1, 1, sub)
            for c in (0, 1):
                at = (sub * 2 + c) * SPAN + ch * PART
                act_out[at:at + PART, :] = v[c * PART:(c + 1) * PART, :].astype(BF)

    ld_g.wait()
    g_pick()
    ld_w.wait()
    for h in both:
        w_p1_hop1(h)
    z_fwd(0, 0, 0)
    z_fwd(0, 0, 1)
    for h in both:
        w_p2_hop1(h, 0)
    for h in both:
        w_p1_hop2(h)
    q_acc[...] = jnp.zeros_like(q_acc)
    for h in both:
        w_p2_hop1(h, -1)
        w_p2_hop1(h, 1)
    z_fwd(0, 1, 0)
    for h in both:
        w_p2_hop2(h, 0)
    z_fwd(0, 1, 1)
    for h in both:
        w_p2_hop1(h, 2)
    g_copies = g_out()
    for h in both:
        w_p2_hop2(h, -1)
        w_p2_hop2(h, 1)
    z_fwd(0, 2, 0)
    z_fwd(1, 0, 0)
    for h in both:
        w_p2_hop2(h, 2)
    z_fwd(0, 2, 1)
    z_fwd(1, 0, 1)
    for d in sib_w:
        d.wait_recv()
    for k in (0, 1, -1, 2, -2, 3, -3):
        add_q(0, mod8(z + k))
    z_fwd(0, 3, 0)
    z_fwd(0, 3, 1)
    add_q(0, mod8(z + 4))
    q_out(0)
    z_fwd(1, 1, 0)
    z_fwd(1, 1, 1)
    ld_kv.wait()
    for k in range(1, 8):
        g_copies[k].wait_recv()
    lax.fori_loop(0, 8, pg_step, 0)
    z_fwd(1, 2, 0)
    attend(0, 0, 4)
    z_fwd(1, 2, 1)
    for k in (0, 1, -1, 2, -2, 3, -3):
        add_q(1, mod8(z + k))
    dq_in(0)
    z_start(0)
    z_fwd(1, 3, 0)
    z_fwd(1, 3, 1)
    add_q(1, mod8(z + 4))
    q_out(1)
    for k in (0, 1, -1, 2):
        turn(mod8(z + k))
    z_add(0, 4, 0)
    for k in (-2, 3, -3, 4):
        turn(mod8(z + k))
    attend(1, 0, 3)
    z_add(0, 3, 1)
    attend(1, 3, 4)

    def kv_steps(first, last):
        lax.fori_loop(first, last, kv_step, 0)

    kv_steps(0, 3)
    z_add(0, 3, 0)
    dq_in(1)

    order = [(kx, 2) for kx in (2, 1, 3, 0)] + [(2, ky) for ky in (1, 3, 0)]
    order += [(kx, ky) for kx in (1, 3, 0) for ky in (1, 3, 0)]

    def part_w(kx, ky, c):
        rows = pl.ds(pl.multiple_of(mod4(y + ky) * BLK, BLK), BLK)
        return dot(act_t[mod4(x + kx) * 2 + c, rows], dq_v[...], NN)

    sib_d = {}

    def sib_push(n):
        kx, ky = order[n]
        sib_send[n] = part_w(kx, ky, 1 - core).astype(BF)
        sib_d[kx, ky] = (push(sib_send.at[n], red.at[n], sib), n)

    def red_at(h, kf, ku, off, n):
        kx, ky = (kf, ku) if h == 0 else (ku, kf)
        return red.at[order.index((kx % 4, ky % 4)), pl.ds(h * HALF + off, n)]

    def pair_sum(kx, ky):
        copy, n = sib_d[kx, ky]
        copy.wait_recv()
        red[n] = (red[n].astype(F32) + part_w(kx, ky, core)).astype(BF)

    first_ax = {0: y_dev, 1: x_dev}
    second_ax = {0: x_dev, 1: y_dev}
    c1q, c1h, c2q, c2h = {}, {}, {}, {}

    def quarter1(h, kf):
        c1q[h, 1, kf] = push(red_at(h, kf, 2, 0, QUART), p1q.at[h, 0, kf], first_ax[h][1])
        c1q[h, -1, kf] = push(red_at(h, kf, 2, QUART, QUART), p1q.at[h, 1, kf], first_ax[h][-1])

    def half1(h, kf):
        for e, d in enumerate((1, -1)):
            c1q[h, d, kf].wait_recv()
            src = red_at(h, kf, d, 0, HALF)
            got = p1q[h, e, kf].astype(F32)
            lo = src[:QUART].astype(F32)
            hi = src[QUART:].astype(F32)
            lo, hi = (lo + got, hi) if d == 1 else (lo, hi + got)
            s1h[h, e, kf, :QUART] = lo.astype(BF)
            s1h[h, e, kf, QUART:] = hi.astype(BF)
            c1h[h, d, kf] = push(s1h.at[h, e, kf], p1h.at[h, e, kf], first_ax[h][d])

    def final1(h, kf):
        for d in (1, -1):
            c1h[h, d, kf].wait_recv()
        v = red_at(h, kf, 0, 0, HALF)[...].astype(F32)
        v = v + p1h[h, 0, kf].astype(F32) + p1h[h, 1, kf].astype(F32)
        if kf == 2:
            f1b[h] = v.astype(BF)
            c2q[h, 1] = push(f1b.at[h, pl.ds(0, QUART)], p2q.at[h, 0], second_ax[h][1])
            c2q[h, -1] = push(f1b.at[h, pl.ds(QUART, QUART)], p2q.at[h, 1], second_ax[h][-1])
        else:
            f1[h, kf] = v

    def half2(h):
        for e, d in enumerate((1, -1)):
            c2q[h, d].wait_recv()
            got = p2q[h, e].astype(F32)
            lo = f1[h, d % 4, :QUART]
            hi = f1[h, d % 4, QUART:]
            lo, hi = (lo + got, hi) if d == 1 else (lo, hi + got)
            s2h[h, e, :QUART] = lo.astype(BF)
            s2h[h, e, QUART:] = hi.astype(BF)
            c2h[h, d] = push(s2h.at[h, e], p2h.at[h, e], second_ax[h][d])

    def final2(h):
        for d in (1, -1):
            c2h[h, d].wait_recv()
        w_out[h * HALF:(h + 1) * HALF, :] = (
            f1[h, 0] + p2h[h, 0].astype(F32) + p2h[h, 1].astype(F32)
        )

    def sums(first, last):
        for n in range(first, last):
            kx, ky = order[n]
            pair_sum(kx, ky)
            if ky == 2:
                quarter1(0, kx)
            if kx == 2:
                quarter1(1, ky)

    def halves1(kf):
        for h in both:
            half1(h, kf)

    for n in range(7):
        sib_push(n)
    z_add(0, 2, 1)
    sums(0, 4)
    z_add(0, 2, 0)
    z_start(1)
    sums(4, 7)
    for n in range(7, 16):
        sib_push(n)
    halves1(2)
    sums(7, 12)
    z_add(1, 4, 0)
    halves1(1)
    sums(12, 16)
    z_add(1, 3, 1)
    halves1(3)
    halves1(0)
    for h in both:
        final1(h, 2)
    z_end(0)
    z_add(1, 3, 0)
    for h in both:
        final1(h, 1)
    z_add(1, 2, 1)
    for h in both:
        final1(h, 3)
    for h in both:
        half2(h)
    z_add(1, 2, 0)
    for h in both:
        final1(h, 0)
    kv_steps(3, 8)
    for h in both:
        final2(h)
    out_w = pltpu.make_async_copy(w_out, w_o, out_sems.at[0])
    out_w.start()
    z_end(1)
    out_act = pltpu.make_async_copy(act_out, act_o, out_sems.at[1])
    out_act.start()

    for d in sends:
        d.wait_send()
    out_w.wait()
    out_act.wait()
    for k in range(8):
        if k:
            for ch in both:
                dq_copy(ch, k, sib["seq"]).wait_send()
        kv_copy(k).wait()


def tail(act_ref, w_ref, kv_ref, act_out, w_out, kv_out, act_v, w_v, kv_v, in_sems, out_sems):
    moves = [(act_ref, act_v, act_out), (w_ref, w_v, w_out)]
    moves += [(kv_ref.at[j], kv_v.at[j], kv_out.at[j]) for j in range(kv_v.shape[0])]
    come = [
        pltpu.make_async_copy(src, mid, in_sems.at[n]) for n, (src, mid, _) in enumerate(moves)
    ]
    go = [
        pltpu.make_async_copy(mid, dst, out_sems.at[n]) for n, (_, mid, dst) in enumerate(moves)
    ]
    for copy in come:
        copy.start()
    for first, second in zip(come, go):
        first.wait()
        second.start()
    for copy in go:
        copy.wait()


def on_device(span_act, q_weight, out_grad, neighbour_kv, neighbour_ids, owner):
    tok, width = out_grad.shape
    dcol = span_act.shape[1]
    half, quart = tok // 2, tok // 4
    any_spec = pl.BlockSpec(memory_space=pl.ANY)
    vmem = pl.BlockSpec(memory_space=pltpu.VMEM)
    hbm = pl.BlockSpec(memory_space=pltpu.HBM)

    def bf(*shape):
        return pltpu.VMEM(shape, BF)

    def f32(*shape):
        return pltpu.VMEM(shape, F32)

    shapes = (
        jax.ShapeDtypeStruct((tok, dcol), BF),
        jax.ShapeDtypeStruct((q_weight.shape[0], width), F32),
        jax.ShapeDtypeStruct(neighbour_kv.shape, BF),
    )
    results = pl.pallas_call(
        kernel,
        out_shape=shapes,
        in_specs=[any_spec, any_spec, any_spec, any_spec, vmem,
                  pl.BlockSpec(memory_space=pltpu.SMEM)],
        out_specs=(any_spec,) * 3,
        scratch_shapes=[
            bf(tok, dcol), f32(tok, width),
            bf(8, tok, dcol), bf(8, dcol, tok), bf(8, dcol, width),
            bf(*neighbour_kv.shape), f32(8, 2, width // HD * SPAN // 2, KEYS), bf(8, width // HD, SPAN, KEYS), bf(8, width // HD, SPAN, KEYS),
            bf(tok, width), f32(tok, width), bf(tok, width),
            bf(2, 8, SPAN // 2, width), bf(8, SPAN, width), bf(8, SPAN, width), bf(8, SPAN, width),
            bf(8, SPAN, width), bf(8, SPAN, width), bf(tok, width),
            bf(28, quart, dcol), bf(28, quart, dcol), f32(2, 2, 2, quart, dcol),
            bf(16, tok, width), bf(16, tok, width),
            bf(2, 2, 4, quart, width), bf(2, 2, 4, half, width), bf(2, 2, 4, half, width),
            f32(2, 4, half, width), bf(2, half, width), bf(2, 2, half, width),
            bf(2, 2, quart, width), bf(2, 2, half, width),
            pltpu.SemaphoreType.DMA((200,)), pltpu.SemaphoreType.DMA((200,)),
            *[pltpu.SemaphoreType.DMA((8,))] * 2, *[pltpu.SemaphoreType.DMA((2, 8))] * 4,
            pltpu.SemaphoreType.DMA((11,)), pltpu.SemaphoreType.DMA((8,)),
            pltpu.SemaphoreType.DMA((2,)),
        ],
        compiler_params=pltpu.CompilerParams(
            collective_id=0, has_side_effects=True, vmem_limit_bytes=60 * 1024 * 1024
        ),
        cost_estimate=pl.CostEstimate(
            flops=8 * 10**9, bytes_accessed=16 * 2**20, transcendentals=600000
        ),
    )(span_act, q_weight, out_grad, neighbour_kv, neighbour_ids, owner)
    return pl.pallas_call(
        tail,
        out_shape=shapes,
        in_specs=[hbm] * 3,
        out_specs=(hbm,) * 3,
        scratch_shapes=[
            bf(tok, dcol), f32(q_weight.shape[0], width), bf(*neighbour_kv.shape),
            pltpu.SemaphoreType.DMA((10,)), pltpu.SemaphoreType.DMA((10,)),
        ],
        compiler_params=pltpu.CompilerParams(vmem_limit_bytes=60 * 1024 * 1024),
    )(*results)


def solution(mesh):
    in_specs = (
        P(("seq", "dp"), "tensor"),
        P(("seq", "dp"), "tensor"),
        P(("seq", "dp"), "tensor"),
        P(("seq", "dp"), None, None, "tensor"),
        P(("seq", "dp"), None),
        P(),
    )
    out_specs = (
        P(("seq", "dp"), "tensor"),
        P(("seq", "dp"), "tensor"),
        P(("seq", "dp"), None, None, "tensor"),
    )
    return jax.shard_map(
        on_device, mesh=mesh, in_specs=in_specs, out_specs=out_specs, check_vma=False
    )
```

```python
import functools

import jax
import jax.numpy as jnp
from jax import lax
from jax.experimental import pallas as pl
from jax.experimental.pallas import tpu as pltpu
from jax.sharding import PartitionSpec as P

HD = 128
SPAN = 64
KEYS = 256
MESH = pl.DeviceIdType.MESH
BF = jnp.bfloat16
F32 = jnp.float32
NN = (((1,), (0,)), ((), ()))
NT = (((1,), (1,)), ((), ()))
TN = (((0,), (0,)), ((), ()))


def dot(a, b, dims):
    return lax.dot_general(a, b, dims, preferred_element_type=F32)


def kernel(
    act_ref, w_ref, g_ref, kv_ref, ids_ref, owner_ref,
    act_o, w_o, kv_out,
    act_out, w_out,
    act_full, act_t, w_full, kv_v, pg_v, probs_v, sg_v, g_v, q_acc, q_v,
    q_send, q_recv, g_send, g_recv, dq_send, dq_recv, dq_v,
    z_send, z_recv, pend, sib_send, red, p1q, p1h, s1h, f1, f1b, s2h, p2q, p2h,
    send_sems, recv_sems, g_ssem, g_rsem, q_ssem, q_rsem, dq_ssem, dq_rsem, loc_sems, kv_sems, out_sems,
):
    s = lax.axis_index("seq")
    z = lax.axis_index("tensor")
    y = lax.axis_index("dp")
    x = s // 2
    core = s % 2
    TOK = g_v.shape[0]
    HALF = TOK // 2
    QUART = HALF // 2
    BLK = w_ref.shape[0]

    def mod4(v):
        return lax.rem(v + 4, 4)

    def mod8(v):
        return lax.rem(v + 8, 8)

    z_dev = {1: {"tensor": mod8(z + 1)}, -1: {"tensor": mod8(z - 1)}}
    x_dev = {1: {"seq": mod4(x + 1) * 2 + core}, -1: {"seq": mod4(x - 1) * 2 + core}}
    y_dev = {1: {"dp": mod4(y + 1)}, -1: {"dp": mod4(y - 1)}}
    sib = {"seq": s + 1 - 2 * core}

    barrier = pltpu.get_barrier_semaphore()
    partners = [z_dev[1], z_dev[-1], y_dev[1], y_dev[-1]]
    partners += [{"seq": mod8(s + k)} for k in range(1, 8)]
    for dev in partners:
        pl.semaphore_signal(barrier, inc=1, device_id=dev, device_id_type=MESH)

    loads = []

    def load(src, dst):
        d = pltpu.make_async_copy(src, dst, loc_sems.at[len(loads)])
        d.start()
        loads.append(d)
        return d

    own_rows = pl.ds(pl.multiple_of(y * BLK, BLK), BLK)
    PART = SPAN // 2
    ld_act = [
        load(
            act_ref.at[pl.ds(c * SPAN + ch * PART, PART)],
            act_full.at[z, pl.ds(ch * HALF + c * PART, PART)],
        )
        for ch in (0, 1) for c in range(4)
    ]
    ld_w = load(w_ref, w_full.at[s, own_rows])
    ld_g = load(g_ref, g_v)
    ld_kv = load(kv_ref, kv_v)
    pl.semaphore_wait(barrier, len(partners))

    sends = []
    used = []

    def push(src, dst, dev):
        n = len(used)
        used.append(n)
        d = pltpu.make_async_remote_copy(
            src_ref=src, dst_ref=dst, send_sem=send_sems.at[n], recv_sem=recv_sems.at[n],
            device_id=dev, device_id_type=MESH,
        )
        d.start()
        sends.append(d)
        return d

    def act_rows(ch, sub):
        return pl.ds(ch * HALF + sub * QUART, QUART)

    zf = {}

    def z_first(ch):
        for sub in (0, 1):
            if ch == 0:
                for d in (1, -1):
                    zf[d, 0, ch, sub] = [
                        push(
                            act_ref.at[pl.ds(c * SPAN, PART)],
                            act_full.at[z, pl.ds(c * PART, PART)], z_dev[d],
                        )
                        for c in (2 * sub, 2 * sub + 1)
                    ]
            else:
                ref = act_full.at[z, act_rows(ch, sub)]
                for d in (1, -1):
                    zf[d, 0, ch, sub] = [push(ref, ref, z_dev[d])]

    def z_fwd(ch, t, sub):
        for d in (1, -1):
            if (d, t, ch, sub) not in zf:
                continue
            for copy in zf[d, t, ch, sub]:
                copy.wait_recv()
            if t < 2 or (t == 2 and sub == (0 if d == 1 else 1)):
                ref = act_full.at[mod8(z - d * (t + 1)), act_rows(ch, sub)]
                zf[d, t + 1, ch, sub] = [push(ref, ref, z_dev[d])]

    def w_ref_at(h, k1, k2, off, n, c=None):
        dx, dy = (k1, k2) if h == 0 else (k2, k1)
        seq = mod4(x + dx) * 2 + (core if c is None else c)
        return w_full.at[seq, pl.ds(pl.multiple_of(mod4(y + dy) * BLK + h * HALF + off, QUART), n)]

    ax = {0: (x_dev, y_dev), 1: (y_dev, x_dev)}
    sib_w = []

    def to_sib(h, k1, k2):
        ref = w_ref_at(h, k1, k2, 0, HALF)
        sib_w.append(push(ref, ref, sib))

    wp1, wp1b, wp2, wp2b = {}, {}, {}, {}

    def w_start_p1(h):
        src = w_ref_at(h, 0, 0, 0, HALF)
        for d in (1, -1):
            wp1[h, d] = push(src, w_ref_at(h, 0, 0, 0, HALF), ax[h][0][d])

    def w_start_p2(h):
        src = w_ref_at(h, 0, 0, 0, HALF)
        for d in (1, -1):
            wp2[h, 0, d] = push(src, w_ref_at(h, 0, 0, 0, HALF), ax[h][1][d])

    def w_p2_send(h, k):
        ref = w_ref_at(h, k, 0, 0, HALF)
        for d in (1, -1):
            wp2[h, k, d] = push(ref, ref, ax[h][1][d])

    def w_p1_hop1(h):
        for d in (1, -1):
            wp1[h, d].wait_recv()
            ref = w_ref_at(h, -d, 0, 0 if d == 1 else QUART, QUART)
            wp1b[h, d] = push(ref, ref, ax[h][0][d])
            w_p2_send(h, -d)
            to_sib(h, -d, 0)

    def w_p1_hop2(h):
        for d in (1, -1):
            wp1b[h, d].wait_recv()
        w_p2_send(h, 2)
        to_sib(h, 2, 0)

    def w_p2_hop1(h, k):
        for d in (1, -1):
            wp2[h, k, d].wait_recv()
            ref = w_ref_at(h, k, -d, 0 if d == 1 else QUART, QUART)
            wp2b[h, k, d] = push(ref, ref, ax[h][1][d])
            to_sib(h, k, -d)

    def w_p2_hop2(h, k):
        for d in (1, -1):
            wp2b[h, k, d].wait_recv()
        to_sib(h, k, 2)

    both = (0, 1)
    z_first(0)
    ld_w.wait()
    for h in both:
        w_start_p1(h)
    for h in both:
        w_start_p2(h)
    for d in ld_act:
        d.wait()
    z_first(1)
    sib_w.append(push(w_full.at[s, own_rows], w_full.at[s, own_rows], sib))

    block = s * 4 + y
    names = [owner_ref[block * 4 + c] for c in range(4)]

    def peer(dx, dc):
        return mod4(x + dx) * 2 + lax.rem(core + dc, 2)

    def owner_copy(send, recv, ssem, rsem, k, dev):
        return pltpu.make_async_remote_copy(
            src_ref=send, dst_ref=recv, send_sem=ssem.at[k], recv_sem=rsem.at[k],
            device_id={"seq": dev}, device_id_type=MESH,
        )

    def picked(rows, o):
        v = jnp.zeros(rows[0].shape, BF)
        for c in range(4):
            v = jnp.where(names[c] == o, rows[c], v)
        return v

    def g_pick():
        rows = [g_v[c * SPAN:(c + 1) * SPAN, :] for c in range(4)]
        for dx in range(4):
            for dc in (0, 1):
                o, k = peer(dx, dc), dx * 2 + dc
                if k == 0:
                    g_recv[s] = picked(rows, o)
                else:
                    g_send[k] = picked(rows, o)

    def g_out():
        copies = {}
        for k in (4, 5, 2, 3, 6, 7, 1):
            o = peer(k // 2, k % 2)
            copies[k] = owner_copy(g_send.at[k], g_recv.at[s], g_ssem, g_rsem, k, o)
            copies[k].start()
            sends.append(copies[k])
        return copies

    def q_out(ch):
        rows = [
            q_acc[ch * HALF + c * PART:ch * HALF + (c + 1) * PART, :].astype(BF) for c in range(4)
        ]
        for dx in (2, 1, 3, 0):
            for dc in (0, 1):
                o, k = peer(dx, dc), dx * 2 + dc
                if k == 0:
                    q_recv[s, ch * PART:(ch + 1) * PART, :] = picked(rows, o)
                else:
                    q_send[ch, k] = picked(rows, o)
                    copy = owner_copy(
                        q_send.at[ch, k], q_recv.at[s, pl.ds(ch * PART, PART)],
                        q_ssem.at[ch], q_rsem.at[ch], k, o,
                    )
                    copy.start()
                    sends.append(copy)

    def turn(slot):
        act_t[slot] = jnp.transpose(act_full[slot])

    def add_q(ch, slot):
        rows = pl.ds(ch * HALF, HALF)
        q_acc[rows, :] += dot(act_full[slot, rows], w_full[slot], NN)

    scale = HD ** (-0.5)
    heads = g_v.shape[1] // HD

    def slot_of(i):
        dx = i // 2
        dx = jnp.where(dx == 2, 3, jnp.where(dx == 3, 2, dx))
        dc = lax.rem(i, 2)
        return dx * 2 + dc, mod4(x - dx) * 2 + lax.rem(core + dc, 2)

    def dq_copy(ch, k, j):
        rows = pl.ds(ch * PART, PART)
        return owner_copy(
            dq_send.at[j, rows], dq_recv.at[s, rows], dq_ssem.at[ch], dq_rsem.at[ch], k, j
        )

    def stacked(parts):
        return jnp.concatenate(parts, axis=0)

    def col(h):
        return slice(h * HD, (h + 1) * HD)

    def pg_step(j, carry):
        for h in range(heads):
            v = dot(g_recv[j, :, col(h)], kv_v[j, 1, :, col(h)], NT)
            for ch in both:
                pg_v[j, ch, h * PART:(h + 1) * PART, :] = v[ch * PART:(ch + 1) * PART, :]
        return carry

    def attend_slots(ch, slots):
        rows = slice(ch * PART, (ch + 1) * PART)
        parts = [slice(h * PART, (h + 1) * PART) for h in range(heads)]
        scores = [
            stacked([dot(q_recv[j, rows, col(h)], kv_v[j, 0, :, col(h)], NT) for h in range(heads)])
            for j in slots
        ]
        grads = []
        for j, sc in zip(slots, scores):
            live = ids_ref[pl.ds(j, 1), :] != 0
            sc = jnp.where(live, sc * scale, -1e30)
            ex = jnp.exp(sc - jnp.max(sc, axis=1, keepdims=True))
            pg = pg_v[j, ch]
            recip = 1.0 / jnp.sum(ex, axis=1, keepdims=True)
            center = jnp.sum(ex * pg, axis=1, keepdims=True) * recip
            probs = ex * recip
            grads.append((probs.astype(BF), (probs * (pg - center) * scale).astype(BF)))
        for j, (_, sg) in zip(slots, grads):
            for h in range(heads):
                dq_send[j, rows, col(h)] = dot(sg[parts[h]], kv_v[j, 0, :, col(h)], NN).astype(BF)
        for j, (low, sg) in zip(slots, grads):
            for h in range(heads):
                probs_v[j, h, rows, :] = low[parts[h]]
                sg_v[j, h, rows, :] = sg[parts[h]]

    def attend(ch, first, last):
        def chip_step(i, carry):
            k0, j0 = slot_of(2 * i)
            k1, j1 = slot_of(2 * i + 1)

            def wait(k):
                owner_copy(
                    q_send.at[ch, k], q_recv.at[s, pl.ds(ch * PART, PART)],
                    q_ssem.at[ch], q_rsem.at[ch], k, sib["seq"],
                ).wait_recv()

            @pl.when(i > 0)
            def _():
                wait(k0)

            wait(k1)
            attend_slots(ch, (j0, j1))

            @pl.when(i > 0)
            def _():
                dq_copy(ch, k0, j0).start()

            dq_copy(ch, k1, j1).start()
            return carry

        lax.fori_loop(first, last, chip_step, 0)

    def dq_in(ch):
        mine = slice(ch * PART, (ch + 1) * PART)
        dq_recv[s, mine, :] = dq_send[s, mine, :]
        for k in range(1, 8):
            dq_copy(ch, k, sib["seq"]).wait_recv()
        for c in range(4):
            v = jnp.zeros((PART, g_v.shape[1]), BF)
            for o in range(8):
                v = jnp.where(names[c] == o, dq_recv[o, ch * PART:(ch + 1) * PART, :], v)
            dq_v[ch * HALF + c * PART:ch * HALF + (c + 1) * PART, :] = v

    def kv_copy(j):
        return pltpu.make_async_copy(kv_v.at[j], kv_out.at[j], kv_sems.at[j])

    def kv_step(j, carry):
        for h in range(heads):
            cols = slice(h * HD, (h + 1) * HD)
            kv_v[j, 0, :, cols] = dot(sg_v[j, h], q_recv[j, :, cols], TN).astype(BF)
            kv_v[j, 1, :, cols] = dot(probs_v[j, h], g_recv[j, :, cols], TN).astype(BF)
        kv_copy(j).start()
        return carry

    def part_act(dest, ch):
        return dot(dq_v[ch * HALF:(ch + 1) * HALF, :], w_full[mod8(dest)], NT)

    def sub_of(value, sub):
        return value[sub * QUART:(sub + 1) * QUART, :]

    zb = {}

    def z_push(ch, d, dist, sub, value):
        n = len(zb)
        z_send[n] = value.astype(BF)
        zb[ch, d, dist, sub] = (push(z_send.at[n], z_recv.at[n], z_dev[d]), n)

    def z_got(ch, d, dist, sub):
        copy, n = zb[ch, d, dist, sub]
        copy.wait_recv()
        return z_recv[n].astype(F32)

    def z_start(ch):
        v = part_act(z + 4, ch)
        z_push(ch, 1, 4, 0, sub_of(v, 0))
        z_push(ch, -1, 4, 1, sub_of(v, 1))
        for e, d in enumerate((1, -1)):
            v = part_act(z + 3 * d, ch)
            z_push(ch, d, 3, 1 - e, sub_of(v, 1 - e))
            pend[ch, e, 0] = sub_of(v, e)

    def z_add(ch, dist, sub):
        for e, d in enumerate((1, -1)):
            sb = sub if d == 1 else 1 - sub
            if sub == 1:
                v = part_act(z + d * (dist - 1), ch)
                pend[ch, e, 1] = sub_of(v, sb)
                pend[ch, e, 0] = sub_of(v, 1 - sb)
            z_push(ch, d, dist - 1, sb, z_got(ch, d, dist, sb) + pend[ch, e, sub])

    def z_end(ch):
        own = part_act(z, ch)
        for sub in (1, 0):
            v = sub_of(own, sub) + z_got(ch, 1, 1, sub) + z_got(ch, -1, 1, sub)
            for c in (0, 1):
                at = (sub * 2 + c) * SPAN + ch * PART
                act_out[at:at + PART, :] = v[c * PART:(c + 1) * PART, :].astype(BF)

    ld_g.wait()
    g_pick()
    for h in both:
        w_p1_hop1(h)
    z_fwd(0, 0, 0)
    z_fwd(0, 0, 1)
    for h in both:
        w_p2_hop1(h, 0)
    for h in both:
        w_p1_hop2(h)
    q_acc[...] = jnp.zeros_like(q_acc)
    for h in both:
        w_p2_hop1(h, -1)
        w_p2_hop1(h, 1)
    z_fwd(0, 1, 0)
    for h in both:
        w_p2_hop2(h, 0)
    z_fwd(0, 1, 1)
    for h in both:
        w_p2_hop1(h, 2)
    g_copies = g_out()
    for h in both:
        w_p2_hop2(h, -1)
        w_p2_hop2(h, 1)
    z_fwd(0, 2, 0)
    z_fwd(1, 0, 0)
    for h in both:
        w_p2_hop2(h, 2)
    z_fwd(0, 2, 1)
    z_fwd(1, 0, 1)
    for d in sib_w:
        d.wait_recv()
    for k in (0, 1, -1, 2, -2, 3, -3):
        add_q(0, mod8(z + k))
    z_fwd(0, 3, 0)
    z_fwd(0, 3, 1)
    add_q(0, mod8(z + 4))
    q_out(0)
    z_fwd(1, 1, 0)
    z_fwd(1, 1, 1)
    ld_kv.wait()
    for k in range(1, 8):
        g_copies[k].wait_recv()
    lax.fori_loop(0, 8, pg_step, 0)
    z_fwd(1, 2, 0)
    attend(0, 0, 4)
    z_fwd(1, 2, 1)
    for k in (0, 1, -1, 2, -2, 3, -3):
        add_q(1, mod8(z + k))
    dq_in(0)
    z_start(0)
    z_fwd(1, 3, 0)
    z_fwd(1, 3, 1)
    add_q(1, mod8(z + 4))
    q_out(1)
    for k in (0, 1, -1, 2):
        turn(mod8(z + k))
    z_add(0, 4, 0)
    for k in (-2, 3, -3, 4):
        turn(mod8(z + k))
    attend(1, 0, 3)
    z_add(0, 3, 1)
    attend(1, 3, 4)

    def kv_steps(first, last):
        lax.fori_loop(first, last, kv_step, 0)

    kv_steps(0, 3)
    z_add(0, 3, 0)
    dq_in(1)

    order = [(kx, 2) for kx in (2, 1, 3, 0)] + [(2, ky) for ky in (1, 3, 0)]
    order += [(kx, ky) for kx in (1, 3, 0) for ky in (1, 3, 0)]

    def part_w(kx, ky, c):
        rows = pl.ds(pl.multiple_of(mod4(y + ky) * BLK, BLK), BLK)
        return dot(act_t[mod4(x + kx) * 2 + c, rows], dq_v[...], NN)

    sib_d = {}

    def sib_push(n):
        kx, ky = order[n]
        sib_send[n] = part_w(kx, ky, 1 - core).astype(BF)
        sib_d[kx, ky] = (push(sib_send.at[n], red.at[n], sib), n)

    def red_at(h, kf, ku, off, n):
        kx, ky = (kf, ku) if h == 0 else (ku, kf)
        return red.at[order.index((kx % 4, ky % 4)), pl.ds(h * HALF + off, n)]

    def pair_sum(kx, ky):
        copy, n = sib_d[kx, ky]
        copy.wait_recv()
        red[n] = (red[n].astype(F32) + part_w(kx, ky, core)).astype(BF)

    first_ax = {0: y_dev, 1: x_dev}
    second_ax = {0: x_dev, 1: y_dev}
    c1q, c1h, c2q, c2h = {}, {}, {}, {}

    def quarter1(h, kf):
        c1q[h, 1, kf] = push(red_at(h, kf, 2, 0, QUART), p1q.at[h, 0, kf], first_ax[h][1])
        c1q[h, -1, kf] = push(red_at(h, kf, 2, QUART, QUART), p1q.at[h, 1, kf], first_ax[h][-1])

    def half1(h, kf):
        for e, d in enumerate((1, -1)):
            c1q[h, d, kf].wait_recv()
            src = red_at(h, kf, d, 0, HALF)
            got = p1q[h, e, kf].astype(F32)
            lo = src[:QUART].astype(F32)
            hi = src[QUART:].astype(F32)
            lo, hi = (lo + got, hi) if d == 1 else (lo, hi + got)
            s1h[h, e, kf, :QUART] = lo.astype(BF)
            s1h[h, e, kf, QUART:] = hi.astype(BF)
            c1h[h, d, kf] = push(s1h.at[h, e, kf], p1h.at[h, e, kf], first_ax[h][d])

    def final1(h, kf):
        for d in (1, -1):
            c1h[h, d, kf].wait_recv()
        v = red_at(h, kf, 0, 0, HALF)[...].astype(F32)
        v = v + p1h[h, 0, kf].astype(F32) + p1h[h, 1, kf].astype(F32)
        if kf == 2:
            f1b[h] = v.astype(BF)
            c2q[h, 1] = push(f1b.at[h, pl.ds(0, QUART)], p2q.at[h, 0], second_ax[h][1])
            c2q[h, -1] = push(f1b.at[h, pl.ds(QUART, QUART)], p2q.at[h, 1], second_ax[h][-1])
        else:
            f1[h, kf] = v

    def half2(h):
        for e, d in enumerate((1, -1)):
            c2q[h, d].wait_recv()
            got = p2q[h, e].astype(F32)
            lo = f1[h, d % 4, :QUART]
            hi = f1[h, d % 4, QUART:]
            lo, hi = (lo + got, hi) if d == 1 else (lo, hi + got)
            s2h[h, e, :QUART] = lo.astype(BF)
            s2h[h, e, QUART:] = hi.astype(BF)
            c2h[h, d] = push(s2h.at[h, e], p2h.at[h, e], second_ax[h][d])

    def final2(h):
        for d in (1, -1):
            c2h[h, d].wait_recv()
        w_out[h * HALF:(h + 1) * HALF, :] = (
            f1[h, 0] + p2h[h, 0].astype(F32) + p2h[h, 1].astype(F32)
        )

    def sums(first, last):
        for n in range(first, last):
            kx, ky = order[n]
            pair_sum(kx, ky)
            if ky == 2:
                quarter1(0, kx)
            if kx == 2:
                quarter1(1, ky)

    def halves1(kf):
        for h in both:
            half1(h, kf)

    for n in range(7):
        sib_push(n)
    z_add(0, 2, 1)
    sums(0, 4)
    z_add(0, 2, 0)
    z_start(1)
    sums(4, 7)
    for n in range(7, 16):
        sib_push(n)
    halves1(2)
    sums(7, 12)
    z_add(1, 4, 0)
    halves1(1)
    sums(12, 16)
    z_add(1, 3, 1)
    halves1(3)
    halves1(0)
    for h in both:
        final1(h, 2)
    z_end(0)
    z_add(1, 3, 0)
    for h in both:
        final1(h, 1)
    z_add(1, 2, 1)
    for h in both:
        final1(h, 3)
    for h in both:
        half2(h)
    z_add(1, 2, 0)
    for h in both:
        final1(h, 0)
    kv_steps(3, 8)
    for h in both:
        final2(h)
    out_w = pltpu.make_async_copy(w_out, w_o, out_sems.at[0])
    out_w.start()
    z_end(1)
    out_act = pltpu.make_async_copy(act_out, act_o, out_sems.at[1])
    out_act.start()

    for d in sends:
        d.wait_send()
    out_w.wait()
    out_act.wait()
    for k in range(8):
        if k:
            for ch in both:
                dq_copy(ch, k, sib["seq"]).wait_send()
        kv_copy(k).wait()


def tail(act_ref, w_ref, kv_ref, act_out, w_out, kv_out, act_v, w_v, kv_v, in_sems, out_sems):
    moves = [(act_ref, act_v, act_out), (w_ref, w_v, w_out)]
    moves += [(kv_ref.at[j], kv_v.at[j], kv_out.at[j]) for j in range(kv_v.shape[0])]
    come = [
        pltpu.make_async_copy(src, mid, in_sems.at[n]) for n, (src, mid, _) in enumerate(moves)
    ]
    go = [
        pltpu.make_async_copy(mid, dst, out_sems.at[n]) for n, (_, mid, dst) in enumerate(moves)
    ]
    for copy in come:
        copy.start()
    for first, second in zip(come, go):
        first.wait()
        second.start()
    for copy in go:
        copy.wait()


def on_device(span_act, q_weight, out_grad, neighbour_kv, neighbour_ids, owner):
    tok, width = out_grad.shape
    dcol = span_act.shape[1]
    half, quart = tok // 2, tok // 4
    any_spec = pl.BlockSpec(memory_space=pl.ANY)
    vmem = pl.BlockSpec(memory_space=pltpu.VMEM)
    hbm = pl.BlockSpec(memory_space=pltpu.HBM)

    def bf(*shape):
        return pltpu.VMEM(shape, BF)

    def f32(*shape):
        return pltpu.VMEM(shape, F32)

    shapes = (
        jax.ShapeDtypeStruct((tok, dcol), BF),
        jax.ShapeDtypeStruct((q_weight.shape[0], width), F32),
        jax.ShapeDtypeStruct(neighbour_kv.shape, BF),
    )
    results = pl.pallas_call(
        kernel,
        out_shape=shapes,
        in_specs=[any_spec, any_spec, any_spec, any_spec, vmem,
                  pl.BlockSpec(memory_space=pltpu.SMEM)],
        out_specs=(any_spec,) * 3,
        scratch_shapes=[
            bf(tok, dcol), f32(tok, width),
            bf(8, tok, dcol), bf(8, dcol, tok), bf(8, dcol, width),
            bf(*neighbour_kv.shape), f32(8, 2, width // HD * SPAN // 2, KEYS), bf(8, width // HD, SPAN, KEYS), bf(8, width // HD, SPAN, KEYS),
            bf(tok, width), f32(tok, width), bf(tok, width),
            bf(2, 8, SPAN // 2, width), bf(8, SPAN, width), bf(8, SPAN, width), bf(8, SPAN, width),
            bf(8, SPAN, width), bf(8, SPAN, width), bf(tok, width),
            bf(28, quart, dcol), bf(28, quart, dcol), f32(2, 2, 2, quart, dcol),
            bf(16, tok, width), bf(16, tok, width),
            bf(2, 2, 4, quart, width), bf(2, 2, 4, half, width), bf(2, 2, 4, half, width),
            f32(2, 4, half, width), bf(2, half, width), bf(2, 2, half, width),
            bf(2, 2, quart, width), bf(2, 2, half, width),
            pltpu.SemaphoreType.DMA((200,)), pltpu.SemaphoreType.DMA((200,)),
            *[pltpu.SemaphoreType.DMA((8,))] * 2, *[pltpu.SemaphoreType.DMA((2, 8))] * 4,
            pltpu.SemaphoreType.DMA((11,)), pltpu.SemaphoreType.DMA((8,)),
            pltpu.SemaphoreType.DMA((2,)),
        ],
        compiler_params=pltpu.CompilerParams(
            collective_id=0, has_side_effects=True, vmem_limit_bytes=60 * 1024 * 1024
        ),
        cost_estimate=pl.CostEstimate(
            flops=8 * 10**9, bytes_accessed=16 * 2**20, transcendentals=600000
        ),
    )(span_act, q_weight, out_grad, neighbour_kv, neighbour_ids, owner)
    return pl.pallas_call(
        tail,
        out_shape=shapes,
        in_specs=[hbm] * 3,
        out_specs=(hbm,) * 3,
        scratch_shapes=[
            bf(tok, dcol), f32(q_weight.shape[0], width), bf(*neighbour_kv.shape),
            pltpu.SemaphoreType.DMA((10,)), pltpu.SemaphoreType.DMA((10,)),
        ],
        compiler_params=pltpu.CompilerParams(vmem_limit_bytes=60 * 1024 * 1024),
    )(*results)


def solution(mesh):
    in_specs = (
        P(("seq", "dp"), "tensor"),
        P(("seq", "dp"), "tensor"),
        P(("seq", "dp"), "tensor"),
        P(("seq", "dp"), None, None, "tensor"),
        P(("seq", "dp"), None),
        P(),
    )
    out_specs = (
        P(("seq", "dp"), "tensor"),
        P(("seq", "dp"), "tensor"),
        P(("seq", "dp"), None, None, "tensor"),
    )
    return jax.shard_map(
        on_device, mesh=mesh, in_specs=in_specs, out_specs=out_specs, check_vma=False
    )
```

```python
import functools

import jax
import jax.numpy as jnp
from jax import lax
from jax.experimental import pallas as pl
from jax.experimental.pallas import tpu as pltpu
from jax.sharding import PartitionSpec as P

HD = 128
SPAN = 64
KEYS = 256
MESH = pl.DeviceIdType.MESH
BF = jnp.bfloat16
F32 = jnp.float32
NN = (((1,), (0,)), ((), ()))
NT = (((1,), (1,)), ((), ()))
TN = (((0,), (0,)), ((), ()))


def dot(a, b, dims):
    return lax.dot_general(a, b, dims, preferred_element_type=F32)


def kernel(
    act_ref, w_ref, g_ref, kv_ref, ids_ref, owner_ref,
    act_o, w_o, kv_out,
    act_out, w_out,
    act_full, act_t, w_full, kv_v, pg_v, probs_v, sg_v, g_v, q_acc, q_v,
    q_send, q_recv, g_send, g_recv, dq_send, dq_recv, dq_v,
    z_send, z_recv, pend, sib_send, red, p1q, p1h, s1h, f1, f1b, s2h, p2q, p2h,
    send_sems, recv_sems, g_ssem, g_rsem, q_ssem, q_rsem, dq_ssem, dq_rsem, loc_sems, kv_sems, out_sems,
):
    s = lax.axis_index("seq")
    z = lax.axis_index("tensor")
    y = lax.axis_index("dp")
    x = s // 2
    core = s % 2
    TOK = g_v.shape[0]
    HALF = TOK // 2
    QUART = HALF // 2
    BLK = w_ref.shape[0]

    def mod4(v):
        return lax.rem(v + 4, 4)

    def mod8(v):
        return lax.rem(v + 8, 8)

    z_dev = {1: {"tensor": mod8(z + 1)}, -1: {"tensor": mod8(z - 1)}}
    x_dev = {1: {"seq": mod4(x + 1) * 2 + core}, -1: {"seq": mod4(x - 1) * 2 + core}}
    y_dev = {1: {"dp": mod4(y + 1)}, -1: {"dp": mod4(y - 1)}}
    sib = {"seq": s + 1 - 2 * core}

    barrier = pltpu.get_barrier_semaphore()
    partners = [z_dev[1], z_dev[-1], y_dev[1], y_dev[-1]]
    partners += [{"seq": mod8(s + k)} for k in range(1, 8)]
    for dev in partners:
        pl.semaphore_signal(barrier, inc=1, device_id=dev, device_id_type=MESH)

    loads = []

    def load(src, dst):
        d = pltpu.make_async_copy(src, dst, loc_sems.at[len(loads)])
        d.start()
        loads.append(d)
        return d

    own_rows = pl.ds(pl.multiple_of(y * BLK, BLK), BLK)
    PART = SPAN // 2
    ld_act = [
        load(
            act_ref.at[pl.ds(c * SPAN + ch * PART, PART)],
            act_full.at[z, pl.ds(ch * HALF + c * PART, PART)],
        )
        for ch in (0, 1) for c in range(4)
    ]
    ld_w = load(w_ref, w_full.at[s, own_rows])
    ld_g = load(g_ref, g_v)
    ld_kv = load(kv_ref, kv_v)
    pl.semaphore_wait(barrier, len(partners))

    sends = []
    used = []

    def push(src, dst, dev):
        n = len(used)
        used.append(n)
        d = pltpu.make_async_remote_copy(
            src_ref=src, dst_ref=dst, send_sem=send_sems.at[n], recv_sem=recv_sems.at[n],
            device_id=dev, device_id_type=MESH,
        )
        d.start()
        sends.append(d)
        return d

    def act_rows(ch, sub):
        return pl.ds(ch * HALF + sub * QUART, QUART)

    zf = {}

    def z_first(ch):
        for sub in (0, 1):
            if ch == 0:
                for d in (1, -1):
                    zf[d, 0, ch, sub] = [
                        push(
                            act_ref.at[pl.ds(c * SPAN, PART)],
                            act_full.at[z, pl.ds(c * PART, PART)], z_dev[d],
                        )
                        for c in (2 * sub, 2 * sub + 1)
                    ]
            else:
                ref = act_full.at[z, act_rows(ch, sub)]
                for d in (1, -1):
                    zf[d, 0, ch, sub] = [push(ref, ref, z_dev[d])]

    def z_fwd(ch, t, sub):
        for d in (1, -1):
            if (d, t, ch, sub) not in zf:
                continue
            for copy in zf[d, t, ch, sub]:
                copy.wait_recv()
            if t < 2 or (t == 2 and sub == (0 if d == 1 else 1)):
                ref = act_full.at[mod8(z - d * (t + 1)), act_rows(ch, sub)]
                zf[d, t + 1, ch, sub] = [push(ref, ref, z_dev[d])]

    def w_ref_at(h, k1, k2, off, n, c=None):
        dx, dy = (k1, k2) if h == 0 else (k2, k1)
        seq = mod4(x + dx) * 2 + (core if c is None else c)
        return w_full.at[seq, pl.ds(pl.multiple_of(mod4(y + dy) * BLK + h * HALF + off, QUART), n)]

    ax = {0: (x_dev, y_dev), 1: (y_dev, x_dev)}
    sib_w = []

    def to_sib(h, k1, k2):
        ref = w_ref_at(h, k1, k2, 0, HALF)
        sib_w.append(push(ref, ref, sib))

    wp1, wp1b, wp2, wp2b = {}, {}, {}, {}

    def w_start_p1(h):
        src = w_ref_at(h, 0, 0, 0, HALF)
        for d in (1, -1):
            wp1[h, d] = push(src, w_ref_at(h, 0, 0, 0, HALF), ax[h][0][d])

    def w_start_p2(h):
        src = w_ref_at(h, 0, 0, 0, HALF)
        for d in (1, -1):
            wp2[h, 0, d] = push(src, w_ref_at(h, 0, 0, 0, HALF), ax[h][1][d])

    def w_p2_send(h, k):
        ref = w_ref_at(h, k, 0, 0, HALF)
        for d in (1, -1):
            wp2[h, k, d] = push(ref, ref, ax[h][1][d])

    def w_p1_hop1(h):
        for d in (1, -1):
            wp1[h, d].wait_recv()
            ref = w_ref_at(h, -d, 0, 0 if d == 1 else QUART, QUART)
            wp1b[h, d] = push(ref, ref, ax[h][0][d])
            w_p2_send(h, -d)
            to_sib(h, -d, 0)

    def w_p1_hop2(h):
        for d in (1, -1):
            wp1b[h, d].wait_recv()
        w_p2_send(h, 2)
        to_sib(h, 2, 0)

    def w_p2_hop1(h, k):
        for d in (1, -1):
            wp2[h, k, d].wait_recv()
            ref = w_ref_at(h, k, -d, 0 if d == 1 else QUART, QUART)
            wp2b[h, k, d] = push(ref, ref, ax[h][1][d])
            to_sib(h, k, -d)

    def w_p2_hop2(h, k):
        for d in (1, -1):
            wp2b[h, k, d].wait_recv()
        to_sib(h, k, 2)

    both = (0, 1)
    z_first(0)
    ld_w.wait()
    for h in both:
        w_start_p1(h)
    for h in both:
        w_start_p2(h)
    for d in ld_act:
        d.wait()
    z_first(1)
    sib_w.append(push(w_full.at[s, own_rows], w_full.at[s, own_rows], sib))

    block = s * 4 + y
    names = [owner_ref[block * 4 + c] for c in range(4)]

    def peer(dx, dc):
        return mod4(x + dx) * 2 + lax.rem(core + dc, 2)

    def owner_copy(send, recv, ssem, rsem, k, dev):
        return pltpu.make_async_remote_copy(
            src_ref=send, dst_ref=recv, send_sem=ssem.at[k], recv_sem=rsem.at[k],
            device_id={"seq": dev}, device_id_type=MESH,
        )

    def picked(rows, o):
        v = jnp.zeros(rows[0].shape, BF)
        for c in range(4):
            v = jnp.where(names[c] == o, rows[c], v)
        return v

    def g_pick():
        rows = [g_v[c * SPAN:(c + 1) * SPAN, :] for c in range(4)]
        for dx in range(4):
            for dc in (0, 1):
                o, k = peer(dx, dc), dx * 2 + dc
                if k == 0:
                    g_recv[s] = picked(rows, o)
                else:
                    g_send[k] = picked(rows, o)

    def g_out():
        copies = {}
        for k in (4, 5, 2, 3, 6, 7, 1):
            o = peer(k // 2, k % 2)
            copies[k] = owner_copy(g_send.at[k], g_recv.at[s], g_ssem, g_rsem, k, o)
            copies[k].start()
            sends.append(copies[k])
        return copies

    def q_out(ch):
        rows = [
            q_acc[ch * HALF + c * PART:ch * HALF + (c + 1) * PART, :].astype(BF) for c in range(4)
        ]
        for dx in (2, 1, 3, 0):
            for dc in (0, 1):
                o, k = peer(dx, dc), dx * 2 + dc
                if k == 0:
                    q_recv[s, ch * PART:(ch + 1) * PART, :] = picked(rows, o)
                else:
                    q_send[ch, k] = picked(rows, o)
                    copy = owner_copy(
                        q_send.at[ch, k], q_recv.at[s, pl.ds(ch * PART, PART)],
                        q_ssem.at[ch], q_rsem.at[ch], k, o,
                    )
                    copy.start()
                    sends.append(copy)

    def turn(slot):
        act_t[slot] = jnp.transpose(act_full[slot])

    def add_q(ch, slot):
        rows = pl.ds(ch * HALF, HALF)
        q_acc[rows, :] += dot(act_full[slot, rows], w_full[slot], NN)

    scale = HD ** (-0.5)
    heads = g_v.shape[1] // HD

    def slot_of(i):
        dx = i // 2
        dx = jnp.where(dx == 2, 3, jnp.where(dx == 3, 2, dx))
        dc = lax.rem(i, 2)
        return dx * 2 + dc, mod4(x - dx) * 2 + lax.rem(core + dc, 2)

    def dq_copy(ch, k, j):
        rows = pl.ds(ch * PART, PART)
        return owner_copy(
            dq_send.at[j, rows], dq_recv.at[s, rows], dq_ssem.at[ch], dq_rsem.at[ch], k, j
        )

    def stacked(parts):
        return jnp.concatenate(parts, axis=0)

    def col(h):
        return slice(h * HD, (h + 1) * HD)

    def pg_step(j, carry):
        for h in range(heads):
            v = dot(g_recv[j, :, col(h)], kv_v[j, 1, :, col(h)], NT)
            for ch in both:
                pg_v[j, ch, h * PART:(h + 1) * PART, :] = v[ch * PART:(ch + 1) * PART, :]
        return carry

    def attend_slots(ch, slots):
        rows = slice(ch * PART, (ch + 1) * PART)
        parts = [slice(h * PART, (h + 1) * PART) for h in range(heads)]
        scores = [
            stacked([dot(q_recv[j, rows, col(h)], kv_v[j, 0, :, col(h)], NT) for h in range(heads)])
            for j in slots
        ]
        grads = []
        for j, sc in zip(slots, scores):
            live = ids_ref[pl.ds(j, 1), :] != 0
            sc = jnp.where(live, sc * scale, -1e30)
            ex = jnp.exp(sc - jnp.max(sc, axis=1, keepdims=True))
            pg = pg_v[j, ch]
            recip = 1.0 / jnp.sum(ex, axis=1, keepdims=True)
            center = jnp.sum(ex * pg, axis=1, keepdims=True) * recip
            probs = ex * recip
            grads.append((probs.astype(BF), (probs * (pg - center) * scale).astype(BF)))
        for j, (_, sg) in zip(slots, grads):
            for h in range(heads):
                dq_send[j, rows, col(h)] = dot(sg[parts[h]], kv_v[j, 0, :, col(h)], NN).astype(BF)
        for j, (low, sg) in zip(slots, grads):
            for h in range(heads):
                probs_v[j, h, rows, :] = low[parts[h]]
                sg_v[j, h, rows, :] = sg[parts[h]]

    def attend(ch, first, last):
        def chip_step(i, carry):
            k0, j0 = slot_of(2 * i)
            k1, j1 = slot_of(2 * i + 1)

            def wait(k):
                owner_copy(
                    q_send.at[ch, k], q_recv.at[s, pl.ds(ch * PART, PART)],
                    q_ssem.at[ch], q_rsem.at[ch], k, sib["seq"],
                ).wait_recv()

            @pl.when(i > 0)
            def _():
                wait(k0)

            wait(k1)
            attend_slots(ch, (j0, j1))

            @pl.when(i > 0)
            def _():
                dq_copy(ch, k0, j0).start()

            dq_copy(ch, k1, j1).start()
            return carry

        lax.fori_loop(first, last, chip_step, 0)

    def dq_in(ch):
        mine = slice(ch * PART, (ch + 1) * PART)
        dq_recv[s, mine, :] = dq_send[s, mine, :]
        for k in range(1, 8):
            dq_copy(ch, k, sib["seq"]).wait_recv()
        for c in range(4):
            v = jnp.zeros((PART, g_v.shape[1]), BF)
            for o in range(8):
                v = jnp.where(names[c] == o, dq_recv[o, ch * PART:(ch + 1) * PART, :], v)
            dq_v[ch * HALF + c * PART:ch * HALF + (c + 1) * PART, :] = v

    def kv_copy(j):
        return pltpu.make_async_copy(kv_v.at[j], kv_out.at[j], kv_sems.at[j])

    def kv_step(j, carry):
        for h in range(heads):
            cols = slice(h * HD, (h + 1) * HD)
            kv_v[j, 0, :, cols] = dot(sg_v[j, h], q_recv[j, :, cols], TN).astype(BF)
            kv_v[j, 1, :, cols] = dot(probs_v[j, h], g_recv[j, :, cols], TN).astype(BF)
        kv_copy(j).start()
        return carry

    def part_act(dest, ch):
        return dot(dq_v[ch * HALF:(ch + 1) * HALF, :], w_full[mod8(dest)], NT)

    def sub_of(value, sub):
        return value[sub * QUART:(sub + 1) * QUART, :]

    zb = {}

    def z_push(ch, d, dist, sub, value):
        n = len(zb)
        z_send[n] = value.astype(BF)
        zb[ch, d, dist, sub] = (push(z_send.at[n], z_recv.at[n], z_dev[d]), n)

    def z_got(ch, d, dist, sub):
        copy, n = zb[ch, d, dist, sub]
        copy.wait_recv()
        return z_recv[n].astype(F32)

    def z_start(ch):
        v = part_act(z + 4, ch)
        z_push(ch, 1, 4, 0, sub_of(v, 0))
        z_push(ch, -1, 4, 1, sub_of(v, 1))
        for e, d in enumerate((1, -1)):
            v = part_act(z + 3 * d, ch)
            z_push(ch, d, 3, 1 - e, sub_of(v, 1 - e))
            pend[ch, e, 0] = sub_of(v, e)

    def z_add(ch, dist, sub):
        for e, d in enumerate((1, -1)):
            sb = sub if d == 1 else 1 - sub
            if sub == 1:
                v = part_act(z + d * (dist - 1), ch)
                pend[ch, e, 1] = sub_of(v, sb)
                pend[ch, e, 0] = sub_of(v, 1 - sb)
            z_push(ch, d, dist - 1, sb, z_got(ch, d, dist, sb) + pend[ch, e, sub])

    def z_end(ch):
        own = part_act(z, ch)
        for sub in (1, 0):
            v = sub_of(own, sub) + z_got(ch, 1, 1, sub) + z_got(ch, -1, 1, sub)
            for c in (0, 1):
                at = (sub * 2 + c) * SPAN + ch * PART
                act_out[at:at + PART, :] = v[c * PART:(c + 1) * PART, :].astype(BF)

    ld_g.wait()
    g_pick()
    for h in both:
        w_p1_hop1(h)
    z_fwd(0, 0, 0)
    z_fwd(0, 0, 1)
    for h in both:
        w_p2_hop1(h, 0)
    for h in both:
        w_p1_hop2(h)
    q_acc[...] = jnp.zeros_like(q_acc)
    for h in both:
        w_p2_hop1(h, -1)
        w_p2_hop1(h, 1)
    z_fwd(0, 1, 0)
    for h in both:
        w_p2_hop2(h, 0)
    z_fwd(0, 1, 1)
    for h in both:
        w_p2_hop1(h, 2)
    g_copies = g_out()
    for h in both:
        w_p2_hop2(h, -1)
        w_p2_hop2(h, 1)
    z_fwd(0, 2, 0)
    z_fwd(1, 0, 0)
    for h in both:
        w_p2_hop2(h, 2)
    z_fwd(0, 2, 1)
    z_fwd(1, 0, 1)
    for d in sib_w:
        d.wait_recv()
    for k in (0, 1, -1, 2, -2, 3, -3):
        add_q(0, mod8(z + k))
    z_fwd(0, 3, 0)
    z_fwd(0, 3, 1)
    add_q(0, mod8(z + 4))
    q_out(0)
    z_fwd(1, 1, 0)
    ld_kv.wait()
    for k in range(1, 8):
        g_copies[k].wait_recv()
    lax.fori_loop(0, 8, pg_step, 0)
    z_fwd(1, 1, 1)
    attend(0, 0, 2)
    z_fwd(1, 2, 0)
    attend(0, 2, 4)
    z_fwd(1, 2, 1)
    for k in (0, 1, -1, 2, -2, 3, -3):
        add_q(1, mod8(z + k))
    dq_in(0)
    z_start(0)
    z_fwd(1, 3, 0)
    z_fwd(1, 3, 1)
    add_q(1, mod8(z + 4))
    q_out(1)
    for k in (0, 1, -1, 2):
        turn(mod8(z + k))
    z_add(0, 4, 0)
    for k in (-2, 3, -3, 4):
        turn(mod8(z + k))
    attend(1, 0, 3)
    z_add(0, 3, 1)
    attend(1, 3, 4)

    def kv_steps(first, last):
        lax.fori_loop(first, last, kv_step, 0)

    kv_steps(0, 3)
    z_add(0, 3, 0)
    dq_in(1)

    order = [(kx, 2) for kx in (2, 1, 3, 0)] + [(2, ky) for ky in (1, 3, 0)]
    order += [(kx, ky) for kx in (1, 3, 0) for ky in (1, 3, 0)]

    def part_w(kx, ky, c):
        rows = pl.ds(pl.multiple_of(mod4(y + ky) * BLK, BLK), BLK)
        return dot(act_t[mod4(x + kx) * 2 + c, rows], dq_v[...], NN)

    sib_d = {}

    def sib_push(n):
        kx, ky = order[n]
        sib_send[n] = part_w(kx, ky, 1 - core).astype(BF)
        sib_d[kx, ky] = (push(sib_send.at[n], red.at[n], sib), n)

    def red_at(h, kf, ku, off, n):
        kx, ky = (kf, ku) if h == 0 else (ku, kf)
        return red.at[order.index((kx % 4, ky % 4)), pl.ds(h * HALF + off, n)]

    def pair_sum(kx, ky):
        copy, n = sib_d[kx, ky]
        copy.wait_recv()
        red[n] = (red[n].astype(F32) + part_w(kx, ky, core)).astype(BF)

    first_ax = {0: y_dev, 1: x_dev}
    second_ax = {0: x_dev, 1: y_dev}
    c1q, c1h, c2q, c2h = {}, {}, {}, {}

    def quarter1(h, kf):
        c1q[h, 1, kf] = push(red_at(h, kf, 2, 0, QUART), p1q.at[h, 0, kf], first_ax[h][1])
        c1q[h, -1, kf] = push(red_at(h, kf, 2, QUART, QUART), p1q.at[h, 1, kf], first_ax[h][-1])

    def half1(h, kf):
        for e, d in enumerate((1, -1)):
            c1q[h, d, kf].wait_recv()
            src = red_at(h, kf, d, 0, HALF)
            got = p1q[h, e, kf].astype(F32)
            lo = src[:QUART].astype(F32)
            hi = src[QUART:].astype(F32)
            lo, hi = (lo + got, hi) if d == 1 else (lo, hi + got)
            s1h[h, e, kf, :QUART] = lo.astype(BF)
            s1h[h, e, kf, QUART:] = hi.astype(BF)
            c1h[h, d, kf] = push(s1h.at[h, e, kf], p1h.at[h, e, kf], first_ax[h][d])

    def final1(h, kf):
        for d in (1, -1):
            c1h[h, d, kf].wait_recv()
        v = red_at(h, kf, 0, 0, HALF)[...].astype(F32)
        v = v + p1h[h, 0, kf].astype(F32) + p1h[h, 1, kf].astype(F32)
        if kf == 2:
            f1b[h] = v.astype(BF)
            c2q[h, 1] = push(f1b.at[h, pl.ds(0, QUART)], p2q.at[h, 0], second_ax[h][1])
            c2q[h, -1] = push(f1b.at[h, pl.ds(QUART, QUART)], p2q.at[h, 1], second_ax[h][-1])
        else:
            f1[h, kf] = v

    def half2(h):
        for e, d in enumerate((1, -1)):
            c2q[h, d].wait_recv()
            got = p2q[h, e].astype(F32)
            lo = f1[h, d % 4, :QUART]
            hi = f1[h, d % 4, QUART:]
            lo, hi = (lo + got, hi) if d == 1 else (lo, hi + got)
            s2h[h, e, :QUART] = lo.astype(BF)
            s2h[h, e, QUART:] = hi.astype(BF)
            c2h[h, d] = push(s2h.at[h, e], p2h.at[h, e], second_ax[h][d])

    def final2(h):
        for d in (1, -1):
            c2h[h, d].wait_recv()
        w_out[h * HALF:(h + 1) * HALF, :] = (
            f1[h, 0] + p2h[h, 0].astype(F32) + p2h[h, 1].astype(F32)
        )

    def sums(first, last):
        for n in range(first, last):
            kx, ky = order[n]
            pair_sum(kx, ky)
            if ky == 2:
                quarter1(0, kx)
            if kx == 2:
                quarter1(1, ky)

    def halves1(kf):
        for h in both:
            half1(h, kf)

    for n in range(7):
        sib_push(n)
    z_add(0, 2, 1)
    sums(0, 4)
    z_add(0, 2, 0)
    z_start(1)
    sums(4, 7)
    for n in range(7, 16):
        sib_push(n)
    halves1(2)
    sums(7, 12)
    z_add(1, 4, 0)
    halves1(1)
    sums(12, 16)
    z_add(1, 3, 1)
    halves1(3)
    halves1(0)
    for h in both:
        final1(h, 2)
    z_end(0)
    z_add(1, 3, 0)
    for h in both:
        final1(h, 1)
    z_add(1, 2, 1)
    for h in both:
        final1(h, 3)
    for h in both:
        half2(h)
    z_add(1, 2, 0)
    for h in both:
        final1(h, 0)
    kv_steps(3, 8)
    for h in both:
        final2(h)
    out_w = pltpu.make_async_copy(w_out, w_o, out_sems.at[0])
    out_w.start()
    z_end(1)
    out_act = pltpu.make_async_copy(act_out, act_o, out_sems.at[1])
    out_act.start()

    for d in sends:
        d.wait_send()
    out_w.wait()
    out_act.wait()
    for k in range(8):
        if k:
            for ch in both:
                dq_copy(ch, k, sib["seq"]).wait_send()
        kv_copy(k).wait()


def tail(act_ref, w_ref, kv_ref, act_out, w_out, kv_out, act_v, w_v, kv_v, in_sems, out_sems):
    moves = [(act_ref, act_v, act_out), (w_ref, w_v, w_out)]
    moves += [(kv_ref.at[j], kv_v.at[j], kv_out.at[j]) for j in range(kv_v.shape[0])]
    come = [
        pltpu.make_async_copy(src, mid, in_sems.at[n]) for n, (src, mid, _) in enumerate(moves)
    ]
    go = [
        pltpu.make_async_copy(mid, dst, out_sems.at[n]) for n, (_, mid, dst) in enumerate(moves)
    ]
    for copy in come:
        copy.start()
    for first, second in zip(come, go):
        first.wait()
        second.start()
    for copy in go:
        copy.wait()


def on_device(span_act, q_weight, out_grad, neighbour_kv, neighbour_ids, owner):
    tok, width = out_grad.shape
    dcol = span_act.shape[1]
    half, quart = tok // 2, tok // 4
    any_spec = pl.BlockSpec(memory_space=pl.ANY)
    vmem = pl.BlockSpec(memory_space=pltpu.VMEM)
    hbm = pl.BlockSpec(memory_space=pltpu.HBM)

    def bf(*shape):
        return pltpu.VMEM(shape, BF)

    def f32(*shape):
        return pltpu.VMEM(shape, F32)

    shapes = (
        jax.ShapeDtypeStruct((tok, dcol), BF),
        jax.ShapeDtypeStruct((q_weight.shape[0], width), F32),
        jax.ShapeDtypeStruct(neighbour_kv.shape, BF),
    )
    results = pl.pallas_call(
        kernel,
        out_shape=shapes,
        in_specs=[any_spec, any_spec, any_spec, any_spec, vmem,
                  pl.BlockSpec(memory_space=pltpu.SMEM)],
        out_specs=(any_spec,) * 3,
        scratch_shapes=[
            bf(tok, dcol), f32(tok, width),
            bf(8, tok, dcol), bf(8, dcol, tok), bf(8, dcol, width),
            bf(*neighbour_kv.shape), f32(8, 2, width // HD * SPAN // 2, KEYS), bf(8, width // HD, SPAN, KEYS), bf(8, width // HD, SPAN, KEYS),
            bf(tok, width), f32(tok, width), bf(tok, width),
            bf(2, 8, SPAN // 2, width), bf(8, SPAN, width), bf(8, SPAN, width), bf(8, SPAN, width),
            bf(8, SPAN, width), bf(8, SPAN, width), bf(tok, width),
            bf(28, quart, dcol), bf(28, quart, dcol), f32(2, 2, 2, quart, dcol),
            bf(16, tok, width), bf(16, tok, width),
            bf(2, 2, 4, quart, width), bf(2, 2, 4, half, width), bf(2, 2, 4, half, width),
            f32(2, 4, half, width), bf(2, half, width), bf(2, 2, half, width),
            bf(2, 2, quart, width), bf(2, 2, half, width),
            pltpu.SemaphoreType.DMA((200,)), pltpu.SemaphoreType.DMA((200,)),
            *[pltpu.SemaphoreType.DMA((8,))] * 2, *[pltpu.SemaphoreType.DMA((2, 8))] * 4,
            pltpu.SemaphoreType.DMA((11,)), pltpu.SemaphoreType.DMA((8,)),
            pltpu.SemaphoreType.DMA((2,)),
        ],
        compiler_params=pltpu.CompilerParams(
            collective_id=0, has_side_effects=True, vmem_limit_bytes=60 * 1024 * 1024
        ),
        cost_estimate=pl.CostEstimate(
            flops=8 * 10**9, bytes_accessed=16 * 2**20, transcendentals=600000
        ),
    )(span_act, q_weight, out_grad, neighbour_kv, neighbour_ids, owner)
    return pl.pallas_call(
        tail,
        out_shape=shapes,
        in_specs=[hbm] * 3,
        out_specs=(hbm,) * 3,
        scratch_shapes=[
            bf(tok, dcol), f32(q_weight.shape[0], width), bf(*neighbour_kv.shape),
            pltpu.SemaphoreType.DMA((10,)), pltpu.SemaphoreType.DMA((10,)),
        ],
        compiler_params=pltpu.CompilerParams(vmem_limit_bytes=60 * 1024 * 1024),
    )(*results)


def solution(mesh):
    in_specs = (
        P(("seq", "dp"), "tensor"),
        P(("seq", "dp"), "tensor"),
        P(("seq", "dp"), "tensor"),
        P(("seq", "dp"), None, None, "tensor"),
        P(("seq", "dp"), None),
        P(),
    )
    out_specs = (
        P(("seq", "dp"), "tensor"),
        P(("seq", "dp"), "tensor"),
        P(("seq", "dp"), None, None, "tensor"),
    )
    return jax.shard_map(
        on_device, mesh=mesh, in_specs=in_specs, out_specs=out_specs, check_vma=False
    )
```

```python
import functools

import jax
import jax.numpy as jnp
from jax import lax
from jax.experimental import pallas as pl
from jax.experimental.pallas import tpu as pltpu
from jax.sharding import PartitionSpec as P

HD = 128
SPAN = 64
KEYS = 256
MESH = pl.DeviceIdType.MESH
BF = jnp.bfloat16
F32 = jnp.float32
NN = (((1,), (0,)), ((), ()))
NT = (((1,), (1,)), ((), ()))
TN = (((0,), (0,)), ((), ()))


def dot(a, b, dims):
    return lax.dot_general(a, b, dims, preferred_element_type=F32)


def kernel(
    act_ref, w_ref, g_ref, kv_ref, ids_ref, owner_ref,
    act_o, w_o, kv_out,
    act_out, w_out,
    act_full, act_t, w_full, kv_v, pg_v, probs_v, sg_v, g_v, q_acc, q_v,
    q_send, q_recv, g_send, g_recv, dq_send, dq_recv, dq_v,
    z_send, z_recv, pend, sib_send, red, p1q, p1h, s1h, f1, f1b, s2h, p2q, p2h,
    send_sems, recv_sems, g_ssem, g_rsem, q_ssem, q_rsem, dq_ssem, dq_rsem, loc_sems, kv_sems, out_sems,
):
    s = lax.axis_index("seq")
    z = lax.axis_index("tensor")
    y = lax.axis_index("dp")
    x = s // 2
    core = s % 2
    TOK = g_v.shape[0]
    HALF = TOK // 2
    QUART = HALF // 2
    BLK = w_ref.shape[0]

    def mod4(v):
        return lax.rem(v + 4, 4)

    def mod8(v):
        return lax.rem(v + 8, 8)

    z_dev = {1: {"tensor": mod8(z + 1)}, -1: {"tensor": mod8(z - 1)}}
    x_dev = {1: {"seq": mod4(x + 1) * 2 + core}, -1: {"seq": mod4(x - 1) * 2 + core}}
    y_dev = {1: {"dp": mod4(y + 1)}, -1: {"dp": mod4(y - 1)}}
    sib = {"seq": s + 1 - 2 * core}

    barrier = pltpu.get_barrier_semaphore()
    partners = [z_dev[1], z_dev[-1], y_dev[1], y_dev[-1]]
    partners += [{"seq": mod8(s + k)} for k in range(1, 8)]
    for dev in partners:
        pl.semaphore_signal(barrier, inc=1, device_id=dev, device_id_type=MESH)

    loads = []

    def load(src, dst):
        d = pltpu.make_async_copy(src, dst, loc_sems.at[len(loads)])
        d.start()
        loads.append(d)
        return d

    own_rows = pl.ds(pl.multiple_of(y * BLK, BLK), BLK)
    PART = SPAN // 2
    ld_act = [
        load(
            act_ref.at[pl.ds(c * SPAN + ch * PART, PART)],
            act_full.at[z, pl.ds(ch * HALF + c * PART, PART)],
        )
        for ch in (0, 1) for c in range(4)
    ]
    ld_w = load(w_ref, w_full.at[s, own_rows])
    ld_g = load(g_ref, g_v)
    ld_kv = load(kv_ref, kv_v)
    pl.semaphore_wait(barrier, len(partners))

    sends = []
    used = []

    def push(src, dst, dev):
        n = len(used)
        used.append(n)
        d = pltpu.make_async_remote_copy(
            src_ref=src, dst_ref=dst, send_sem=send_sems.at[n], recv_sem=recv_sems.at[n],
            device_id=dev, device_id_type=MESH,
        )
        d.start()
        sends.append(d)
        return d

    def act_rows(ch, sub):
        return pl.ds(ch * HALF + sub * QUART, QUART)

    zf = {}

    def z_first(ch):
        for sub in (0, 1):
            if ch == 0:
                for d in (1, -1):
                    zf[d, 0, ch, sub] = [
                        push(
                            act_ref.at[pl.ds(c * SPAN, PART)],
                            act_full.at[z, pl.ds(c * PART, PART)], z_dev[d],
                        )
                        for c in (2 * sub, 2 * sub + 1)
                    ]
            else:
                ref = act_full.at[z, act_rows(ch, sub)]
                for d in (1, -1):
                    zf[d, 0, ch, sub] = [push(ref, ref, z_dev[d])]

    def z_fwd(ch, t, sub):
        for d in (1, -1):
            if (d, t, ch, sub) not in zf:
                continue
            for copy in zf[d, t, ch, sub]:
                copy.wait_recv()
            if t < 2 or (t == 2 and sub == (0 if d == 1 else 1)):
                ref = act_full.at[mod8(z - d * (t + 1)), act_rows(ch, sub)]
                zf[d, t + 1, ch, sub] = [push(ref, ref, z_dev[d])]

    def w_ref_at(h, k1, k2, off, n, c=None):
        dx, dy = (k1, k2) if h == 0 else (k2, k1)
        seq = mod4(x + dx) * 2 + (core if c is None else c)
        return w_full.at[seq, pl.ds(pl.multiple_of(mod4(y + dy) * BLK + h * HALF + off, QUART), n)]

    ax = {0: (x_dev, y_dev), 1: (y_dev, x_dev)}
    sib_w = []

    def to_sib(h, k1, k2):
        ref = w_ref_at(h, k1, k2, 0, HALF)
        sib_w.append(push(ref, ref, sib))

    wp1, wp1b, wp2, wp2b = {}, {}, {}, {}

    def w_start_p1(h):
        src = w_ref_at(h, 0, 0, 0, HALF)
        for d in (1, -1):
            wp1[h, d] = push(src, w_ref_at(h, 0, 0, 0, HALF), ax[h][0][d])

    def w_start_p2(h):
        src = w_ref_at(h, 0, 0, 0, HALF)
        for d in (1, -1):
            wp2[h, 0, d] = push(src, w_ref_at(h, 0, 0, 0, HALF), ax[h][1][d])

    def w_p2_send(h, k):
        ref = w_ref_at(h, k, 0, 0, HALF)
        for d in (1, -1):
            wp2[h, k, d] = push(ref, ref, ax[h][1][d])

    def w_p1_hop1(h):
        for d in (1, -1):
            wp1[h, d].wait_recv()
            ref = w_ref_at(h, -d, 0, 0 if d == 1 else QUART, QUART)
            wp1b[h, d] = push(ref, ref, ax[h][0][d])
            w_p2_send(h, -d)
            to_sib(h, -d, 0)

    def w_p1_hop2(h):
        for d in (1, -1):
            wp1b[h, d].wait_recv()
        w_p2_send(h, 2)
        to_sib(h, 2, 0)

    def w_p2_hop1(h, k):
        for d in (1, -1):
            wp2[h, k, d].wait_recv()
            ref = w_ref_at(h, k, -d, 0 if d == 1 else QUART, QUART)
            wp2b[h, k, d] = push(ref, ref, ax[h][1][d])
            to_sib(h, k, -d)

    def w_p2_hop2(h, k):
        for d in (1, -1):
            wp2b[h, k, d].wait_recv()
        to_sib(h, k, 2)

    both = (0, 1)
    z_first(0)
    ld_w.wait()
    for h in both:
        w_start_p1(h)
    for h in both:
        w_start_p2(h)
    for d in ld_act:
        d.wait()
    z_first(1)
    sib_w.append(push(w_full.at[s, own_rows], w_full.at[s, own_rows], sib))

    block = s * 4 + y
    names = [owner_ref[block * 4 + c] for c in range(4)]

    def peer(dx, dc):
        return mod4(x + dx) * 2 + lax.rem(core + dc, 2)

    def owner_copy(send, recv, ssem, rsem, k, dev):
        return pltpu.make_async_remote_copy(
            src_ref=send, dst_ref=recv, send_sem=ssem.at[k], recv_sem=rsem.at[k],
            device_id={"seq": dev}, device_id_type=MESH,
        )

    def picked(rows, o):
        v = jnp.zeros(rows[0].shape, BF)
        for c in range(4):
            v = jnp.where(names[c] == o, rows[c], v)
        return v

    def g_pick():
        rows = [g_v[c * SPAN:(c + 1) * SPAN, :] for c in range(4)]
        for dx in range(4):
            for dc in (0, 1):
                o, k = peer(dx, dc), dx * 2 + dc
                if k == 0:
                    g_recv[s] = picked(rows, o)
                else:
                    g_send[k] = picked(rows, o)

    def g_out():
        copies = {}
        for k in (4, 5, 2, 3, 6, 7, 1):
            o = peer(k // 2, k % 2)
            copies[k] = owner_copy(g_send.at[k], g_recv.at[s], g_ssem, g_rsem, k, o)
            copies[k].start()
            sends.append(copies[k])
        return copies

    def q_out(ch):
        rows = [
            q_acc[ch * HALF + c * PART:ch * HALF + (c + 1) * PART, :].astype(BF) for c in range(4)
        ]
        for dx in (2, 1, 3, 0):
            for dc in (0, 1):
                o, k = peer(dx, dc), dx * 2 + dc
                if k == 0:
                    q_recv[s, ch * PART:(ch + 1) * PART, :] = picked(rows, o)
                else:
                    q_send[ch, k] = picked(rows, o)
                    copy = owner_copy(
                        q_send.at[ch, k], q_recv.at[s, pl.ds(ch * PART, PART)],
                        q_ssem.at[ch], q_rsem.at[ch], k, o,
                    )
                    copy.start()
                    sends.append(copy)

    def turn(slot):
        act_t[slot] = jnp.transpose(act_full[slot])

    def add_q(ch, slot):
        rows = pl.ds(ch * HALF, HALF)
        q_acc[rows, :] += dot(act_full[slot, rows], w_full[slot], NN)

    scale = HD ** (-0.5)
    heads = g_v.shape[1] // HD

    def slot_of(i):
        dx = i // 2
        dx = jnp.where(dx == 2, 3, jnp.where(dx == 3, 2, dx))
        dc = lax.rem(i, 2)
        return dx * 2 + dc, mod4(x - dx) * 2 + lax.rem(core + dc, 2)

    def dq_copy(ch, k, j):
        rows = pl.ds(ch * PART, PART)
        return owner_copy(
            dq_send.at[j, rows], dq_recv.at[s, rows], dq_ssem.at[ch], dq_rsem.at[ch], k, j
        )

    def stacked(parts):
        return jnp.concatenate(parts, axis=0)

    def col(h):
        return slice(h * HD, (h + 1) * HD)

    def pg_step(j, carry):
        for h in range(heads):
            v = dot(g_recv[j, :, col(h)], kv_v[j, 1, :, col(h)], NT)
            for ch in both:
                pg_v[j, ch, h * PART:(h + 1) * PART, :] = v[ch * PART:(ch + 1) * PART, :]
        return carry

    def attend_slots(ch, slots):
        rows = slice(ch * PART, (ch + 1) * PART)
        parts = [slice(h * PART, (h + 1) * PART) for h in range(heads)]
        scores = [
            stacked([dot(q_recv[j, rows, col(h)], kv_v[j, 0, :, col(h)], NT) for h in range(heads)])
            for j in slots
        ]
        grads = []
        for j, sc in zip(slots, scores):
            live = ids_ref[pl.ds(j, 1), :] != 0
            sc = jnp.where(live, sc * scale, -1e30)
            ex = jnp.exp(sc - jnp.max(sc, axis=1, keepdims=True))
            pg = pg_v[j, ch]
            recip = 1.0 / jnp.sum(ex, axis=1, keepdims=True)
            center = jnp.sum(ex * pg, axis=1, keepdims=True) * recip
            probs = ex * recip
            grads.append((probs.astype(BF), (probs * (pg - center) * scale).astype(BF)))
        for j, (_, sg) in zip(slots, grads):
            for h in range(heads):
                dq_send[j, rows, col(h)] = dot(sg[parts[h]], kv_v[j, 0, :, col(h)], NN).astype(BF)
        for j, (low, sg) in zip(slots, grads):
            for h in range(heads):
                probs_v[j, h, rows, :] = low[parts[h]]
                sg_v[j, h, rows, :] = sg[parts[h]]

    def attend(ch, first, last):
        def chip_step(i, carry):
            k0, j0 = slot_of(2 * i)
            k1, j1 = slot_of(2 * i + 1)

            def wait(k):
                owner_copy(
                    q_send.at[ch, k], q_recv.at[s, pl.ds(ch * PART, PART)],
                    q_ssem.at[ch], q_rsem.at[ch], k, sib["seq"],
                ).wait_recv()

            @pl.when(i > 0)
            def _():
                wait(k0)

            wait(k1)
            attend_slots(ch, (j0, j1))

            @pl.when(i > 0)
            def _():
                dq_copy(ch, k0, j0).start()

            dq_copy(ch, k1, j1).start()
            return carry

        lax.fori_loop(first, last, chip_step, 0)

    def dq_in(ch):
        mine = slice(ch * PART, (ch + 1) * PART)
        dq_recv[s, mine, :] = dq_send[s, mine, :]
        for k in range(1, 8):
            dq_copy(ch, k, sib["seq"]).wait_recv()
        for c in range(4):
            v = jnp.zeros((PART, g_v.shape[1]), BF)
            for o in range(8):
                v = jnp.where(names[c] == o, dq_recv[o, ch * PART:(ch + 1) * PART, :], v)
            dq_v[ch * HALF + c * PART:ch * HALF + (c + 1) * PART, :] = v

    def kv_copy(j):
        return pltpu.make_async_copy(kv_v.at[j], kv_out.at[j], kv_sems.at[j])

    def kv_step(j, carry):
        for h in range(heads):
            cols = slice(h * HD, (h + 1) * HD)
            kv_v[j, 0, :, cols] = dot(sg_v[j, h], q_recv[j, :, cols], TN).astype(BF)
            kv_v[j, 1, :, cols] = dot(probs_v[j, h], g_recv[j, :, cols], TN).astype(BF)
        kv_copy(j).start()
        return carry

    def part_act(dest, ch):
        return dot(dq_v[ch * HALF:(ch + 1) * HALF, :], w_full[mod8(dest)], NT)

    def sub_of(value, sub):
        return value[sub * QUART:(sub + 1) * QUART, :]

    zb = {}

    def z_push(ch, d, dist, sub, value):
        n = len(zb)
        z_send[n] = value.astype(BF)
        zb[ch, d, dist, sub] = (push(z_send.at[n], z_recv.at[n], z_dev[d]), n)

    def z_got(ch, d, dist, sub):
        copy, n = zb[ch, d, dist, sub]
        copy.wait_recv()
        return z_recv[n].astype(F32)

    def z_start(ch):
        v = part_act(z + 4, ch)
        z_push(ch, 1, 4, 0, sub_of(v, 0))
        z_push(ch, -1, 4, 1, sub_of(v, 1))
        for e, d in enumerate((1, -1)):
            v = part_act(z + 3 * d, ch)
            z_push(ch, d, 3, 1 - e, sub_of(v, 1 - e))
            pend[ch, e, 0] = sub_of(v, e)

    def z_add(ch, dist, sub):
        for e, d in enumerate((1, -1)):
            sb = sub if d == 1 else 1 - sub
            if sub == 1:
                v = part_act(z + d * (dist - 1), ch)
                pend[ch, e, 1] = sub_of(v, sb)
                pend[ch, e, 0] = sub_of(v, 1 - sb)
            z_push(ch, d, dist - 1, sb, z_got(ch, d, dist, sb) + pend[ch, e, sub])

    def z_end(ch):
        own = part_act(z, ch)
        for sub in (1, 0):
            v = sub_of(own, sub) + z_got(ch, 1, 1, sub) + z_got(ch, -1, 1, sub)
            for c in (0, 1):
                at = (sub * 2 + c) * SPAN + ch * PART
                act_out[at:at + PART, :] = v[c * PART:(c + 1) * PART, :].astype(BF)

    ld_g.wait()
    g_pick()
    for h in both:
        w_p1_hop1(h)
    z_fwd(0, 0, 0)
    z_fwd(0, 0, 1)
    for h in both:
        w_p2_hop1(h, 0)
    for h in both:
        w_p1_hop2(h)
    q_acc[...] = jnp.zeros_like(q_acc)
    for h in both:
        w_p2_hop1(h, -1)
        w_p2_hop1(h, 1)
    z_fwd(0, 1, 0)
    for h in both:
        w_p2_hop2(h, 0)
    z_fwd(0, 1, 1)
    for h in both:
        w_p2_hop1(h, 2)
    g_copies = g_out()
    for h in both:
        w_p2_hop2(h, -1)
        w_p2_hop2(h, 1)
    z_fwd(0, 2, 0)
    z_fwd(1, 0, 0)
    for h in both:
        w_p2_hop2(h, 2)
    z_fwd(0, 2, 1)
    z_fwd(1, 0, 1)
    for d in sib_w:
        d.wait_recv()
    for k in (0, 1, -1, 2, -2, 3, -3):
        add_q(0, mod8(z + k))
    z_fwd(0, 3, 0)
    z_fwd(0, 3, 1)
    add_q(0, mod8(z + 4))
    q_out(0)
    z_fwd(1, 1, 0)
    ld_kv.wait()
    for k in range(1, 8):
        g_copies[k].wait_recv()
    lax.fori_loop(0, 8, pg_step, 0)
    z_fwd(1, 1, 1)
    attend(0, 0, 2)
    z_fwd(1, 2, 0)
    attend(0, 2, 4)
    z_fwd(1, 2, 1)
    for k in (0, 1, -1, 2, -2, 3, -3):
        add_q(1, mod8(z + k))
    dq_in(0)
    z_start(0)
    z_fwd(1, 3, 0)
    z_fwd(1, 3, 1)
    add_q(1, mod8(z + 4))
    q_out(1)
    for k in (0, 1, -1, 2):
        turn(mod8(z + k))
    z_add(0, 4, 0)
    for k in (-2, 3, -3, 4):
        turn(mod8(z + k))
    attend(1, 0, 3)
    z_add(0, 3, 1)
    attend(1, 3, 4)

    def kv_steps(first, last):
        lax.fori_loop(first, last, kv_step, 0)

    kv_steps(0, 3)
    z_add(0, 3, 0)
    dq_in(1)

    order = [(kx, 2) for kx in (2, 1, 3, 0)] + [(2, ky) for ky in (1, 3, 0)]
    order += [(kx, ky) for kx in (1, 3, 0) for ky in (1, 3, 0)]

    def part_w(kx, ky, c):
        rows = pl.ds(pl.multiple_of(mod4(y + ky) * BLK, BLK), BLK)
        return dot(act_t[mod4(x + kx) * 2 + c, rows], dq_v[...], NN)

    sib_d = {}

    def sib_push(n):
        kx, ky = order[n]
        sib_send[n] = part_w(kx, ky, 1 - core).astype(BF)
        sib_d[kx, ky] = (push(sib_send.at[n], red.at[n], sib), n)

    def red_at(h, kf, ku, off, n):
        kx, ky = (kf, ku) if h == 0 else (ku, kf)
        return red.at[order.index((kx % 4, ky % 4)), pl.ds(h * HALF + off, n)]

    def pair_sum(kx, ky):
        copy, n = sib_d[kx, ky]
        copy.wait_recv()
        red[n] = (red[n].astype(F32) + part_w(kx, ky, core)).astype(BF)

    first_ax = {0: y_dev, 1: x_dev}
    second_ax = {0: x_dev, 1: y_dev}
    c1q, c1h, c2q, c2h = {}, {}, {}, {}

    def quarter1(h, kf):
        c1q[h, 1, kf] = push(red_at(h, kf, 2, 0, QUART), p1q.at[h, 0, kf], first_ax[h][1])
        c1q[h, -1, kf] = push(red_at(h, kf, 2, QUART, QUART), p1q.at[h, 1, kf], first_ax[h][-1])

    def half1(h, kf):
        for e, d in enumerate((1, -1)):
            c1q[h, d, kf].wait_recv()
            src = red_at(h, kf, d, 0, HALF)
            got = p1q[h, e, kf].astype(F32)
            lo = src[:QUART].astype(F32)
            hi = src[QUART:].astype(F32)
            lo, hi = (lo + got, hi) if d == 1 else (lo, hi + got)
            s1h[h, e, kf, :QUART] = lo.astype(BF)
            s1h[h, e, kf, QUART:] = hi.astype(BF)
            c1h[h, d, kf] = push(s1h.at[h, e, kf], p1h.at[h, e, kf], first_ax[h][d])

    def final1(h, kf):
        for d in (1, -1):
            c1h[h, d, kf].wait_recv()
        v = red_at(h, kf, 0, 0, HALF)[...].astype(F32)
        v = v + p1h[h, 0, kf].astype(F32) + p1h[h, 1, kf].astype(F32)
        if kf == 2:
            f1b[h] = v.astype(BF)
            c2q[h, 1] = push(f1b.at[h, pl.ds(0, QUART)], p2q.at[h, 0], second_ax[h][1])
            c2q[h, -1] = push(f1b.at[h, pl.ds(QUART, QUART)], p2q.at[h, 1], second_ax[h][-1])
        else:
            f1[h, kf] = v

    def half2(h):
        for e, d in enumerate((1, -1)):
            c2q[h, d].wait_recv()
            got = p2q[h, e].astype(F32)
            lo = f1[h, d % 4, :QUART]
            hi = f1[h, d % 4, QUART:]
            lo, hi = (lo + got, hi) if d == 1 else (lo, hi + got)
            s2h[h, e, :QUART] = lo.astype(BF)
            s2h[h, e, QUART:] = hi.astype(BF)
            c2h[h, d] = push(s2h.at[h, e], p2h.at[h, e], second_ax[h][d])

    def final2(h):
        for d in (1, -1):
            c2h[h, d].wait_recv()
        w_out[h * HALF:(h + 1) * HALF, :] = (
            f1[h, 0] + p2h[h, 0].astype(F32) + p2h[h, 1].astype(F32)
        )

    def sums(first, last):
        for n in range(first, last):
            kx, ky = order[n]
            pair_sum(kx, ky)
            if ky == 2:
                quarter1(0, kx)
            if kx == 2:
                quarter1(1, ky)

    def halves1(kf):
        for h in both:
            half1(h, kf)

    for n in range(4):
        sib_push(n)
    z_add(0, 2, 1)
    for n in range(4, 7):
        sib_push(n)
    sums(0, 4)
    z_add(0, 2, 0)
    z_start(1)
    sums(4, 7)
    for n in range(7, 16):
        sib_push(n)
    halves1(2)
    sums(7, 12)
    z_add(1, 4, 0)
    halves1(1)
    sums(12, 16)
    z_add(1, 3, 1)
    halves1(3)
    halves1(0)
    for h in both:
        final1(h, 2)
    z_end(0)
    z_add(1, 3, 0)
    for h in both:
        final1(h, 1)
    z_add(1, 2, 1)
    for h in both:
        final1(h, 3)
    for h in both:
        half2(h)
    z_add(1, 2, 0)
    for h in both:
        final1(h, 0)
    kv_steps(3, 8)
    for h in both:
        final2(h)
    out_w = pltpu.make_async_copy(w_out, w_o, out_sems.at[0])
    out_w.start()
    z_end(1)
    out_act = pltpu.make_async_copy(act_out, act_o, out_sems.at[1])
    out_act.start()

    for d in sends:
        d.wait_send()
    out_w.wait()
    out_act.wait()
    for k in range(8):
        if k:
            for ch in both:
                dq_copy(ch, k, sib["seq"]).wait_send()
        kv_copy(k).wait()


def tail(act_ref, w_ref, kv_ref, act_out, w_out, kv_out, act_v, w_v, kv_v, in_sems, out_sems):
    moves = [(act_ref, act_v, act_out), (w_ref, w_v, w_out)]
    moves += [(kv_ref.at[j], kv_v.at[j], kv_out.at[j]) for j in range(kv_v.shape[0])]
    come = [
        pltpu.make_async_copy(src, mid, in_sems.at[n]) for n, (src, mid, _) in enumerate(moves)
    ]
    go = [
        pltpu.make_async_copy(mid, dst, out_sems.at[n]) for n, (_, mid, dst) in enumerate(moves)
    ]
    for copy in come:
        copy.start()
    for first, second in zip(come, go):
        first.wait()
        second.start()
    for copy in go:
        copy.wait()


def on_device(span_act, q_weight, out_grad, neighbour_kv, neighbour_ids, owner):
    tok, width = out_grad.shape
    dcol = span_act.shape[1]
    half, quart = tok // 2, tok // 4
    any_spec = pl.BlockSpec(memory_space=pl.ANY)
    vmem = pl.BlockSpec(memory_space=pltpu.VMEM)
    hbm = pl.BlockSpec(memory_space=pltpu.HBM)

    def bf(*shape):
        return pltpu.VMEM(shape, BF)

    def f32(*shape):
        return pltpu.VMEM(shape, F32)

    shapes = (
        jax.ShapeDtypeStruct((tok, dcol), BF),
        jax.ShapeDtypeStruct((q_weight.shape[0], width), F32),
        jax.ShapeDtypeStruct(neighbour_kv.shape, BF),
    )
    results = pl.pallas_call(
        kernel,
        out_shape=shapes,
        in_specs=[any_spec, any_spec, any_spec, any_spec, vmem,
                  pl.BlockSpec(memory_space=pltpu.SMEM)],
        out_specs=(any_spec,) * 3,
        scratch_shapes=[
            bf(tok, dcol), f32(tok, width),
            bf(8, tok, dcol), bf(8, dcol, tok), bf(8, dcol, width),
            bf(*neighbour_kv.shape), f32(8, 2, width // HD * SPAN // 2, KEYS), bf(8, width // HD, SPAN, KEYS), bf(8, width // HD, SPAN, KEYS),
            bf(tok, width), f32(tok, width), bf(tok, width),
            bf(2, 8, SPAN // 2, width), bf(8, SPAN, width), bf(8, SPAN, width), bf(8, SPAN, width),
            bf(8, SPAN, width), bf(8, SPAN, width), bf(tok, width),
            bf(28, quart, dcol), bf(28, quart, dcol), f32(2, 2, 2, quart, dcol),
            bf(16, tok, width), bf(16, tok, width),
            bf(2, 2, 4, quart, width), bf(2, 2, 4, half, width), bf(2, 2, 4, half, width),
            f32(2, 4, half, width), bf(2, half, width), bf(2, 2, half, width),
            bf(2, 2, quart, width), bf(2, 2, half, width),
            pltpu.SemaphoreType.DMA((200,)), pltpu.SemaphoreType.DMA((200,)),
            *[pltpu.SemaphoreType.DMA((8,))] * 2, *[pltpu.SemaphoreType.DMA((2, 8))] * 4,
            pltpu.SemaphoreType.DMA((11,)), pltpu.SemaphoreType.DMA((8,)),
            pltpu.SemaphoreType.DMA((2,)),
        ],
        compiler_params=pltpu.CompilerParams(
            collective_id=0, has_side_effects=True, vmem_limit_bytes=60 * 1024 * 1024
        ),
        cost_estimate=pl.CostEstimate(
            flops=8 * 10**9, bytes_accessed=16 * 2**20, transcendentals=600000
        ),
    )(span_act, q_weight, out_grad, neighbour_kv, neighbour_ids, owner)
    return pl.pallas_call(
        tail,
        out_shape=shapes,
        in_specs=[hbm] * 3,
        out_specs=(hbm,) * 3,
        scratch_shapes=[
            bf(tok, dcol), f32(q_weight.shape[0], width), bf(*neighbour_kv.shape),
            pltpu.SemaphoreType.DMA((10,)), pltpu.SemaphoreType.DMA((10,)),
        ],
        compiler_params=pltpu.CompilerParams(vmem_limit_bytes=60 * 1024 * 1024),
    )(*results)


def solution(mesh):
    in_specs = (
        P(("seq", "dp"), "tensor"),
        P(("seq", "dp"), "tensor"),
        P(("seq", "dp"), "tensor"),
        P(("seq", "dp"), None, None, "tensor"),
        P(("seq", "dp"), None),
        P(),
    )
    out_specs = (
        P(("seq", "dp"), "tensor"),
        P(("seq", "dp"), "tensor"),
        P(("seq", "dp"), None, None, "tensor"),
    )
    return jax.shard_map(
        on_device, mesh=mesh, in_specs=in_specs, out_specs=out_specs, check_vma=False
    )
```
